128 devices in a mesh: dp: 8 (over z, core), seq: 16 (over y, x).
Axes of the slice: x: 4, y: 4, z: 4, core: 2. Of those that a mesh axis runs over, the one named last changes fastest.
Arguments:
- queries: bfloat16 [16, 2048, 2048], P('dp', 'seq'), may hold values from -6 to 6
- d_context: bfloat16 [16, 2048, 2048], P('dp', 'seq'), may hold values from -12 to 12
- database: bfloat16 [2048, 128, 896], P(('dp', 'seq')), may hold values from -6 to 6
- key_weight: bfloat16 [896, 2048], replicated, may hold values from -0.1875 to 0.1875
- value_weight: bfloat16 [896, 2048], replicated, may hold values from -0.1875 to 0.1875
- neighbour_shard: int32 [8, 16, 4, 2], P('dp', 'seq'), may hold values from 0 to 7, all different within a row; in each aligned block of 4 rows (0 to 3, 4 to 7, ..., all dimensions but the last counted through in order) at most 2 rows name the same one
- neighbour_row: int32 [8, 16, 4, 2], P('dp', 'seq'), may hold values from 0 to 15
Outputs:
- context: bfloat16 [16, 2048, 2048], P('dp', 'seq')
- query_grad: bfloat16 [16, 2048, 2048], P('dp', 'seq')
- database_grad: float32 [2048, 128, 896], P(('dp', 'seq'))
- key_weight_grad: float32 [896, 2048], P(('dp', 'seq'))
- value_weight_grad: float32 [896, 2048], P(('dp', 'seq'))
The draws below stay inside these ranges and needn't reach their ends.
Inputs may be any that keep to these rules, and one draw needn't show every extreme that they name: `neighbour_shard`: among the 4 rows of one device (aligned blocks of the first three dimensions taken together), no shard is named more than 2 times, a bound that some block reaches; the 2 neighbours of one block name different shards.
All inputs are finite; a program needn't handle non-finite values.
Results may differ from the reference program's by a relative error of at most 0.015.
Values may be sent and summed in bfloat16 or wider, within the bound.
A program may use at most 192 MiB of HBM per device.

```python
import math
import jax
import jax.numpy as jnp
import numpy as np
from jax import lax

HEADS = 16
HD = 128
ENC = 896
SPAN = 64
NB_LEN = 128
NBR = 2
LEN = 2048
SEQS_DP = 2
HW = 2048
BLOCKS_DEV = 4
CAP = 2
ROWS_DEV = 16
BATCH = 16
DB_ROWS = 2048
N_DP = 8
N_SEQ = 16


def with_ends(array, rng, smallest, high):
    longest = array.shape.index(max(array.shape))
    spots = []
    for shift in (0, 1):
        where = [jax.random.randint(jax.random.fold_in(rng, axis), (), 0, length) for axis, length in enumerate(array.shape)]
        where[longest] = (where[longest] + shift) % array.shape[longest]
        spots.append(tuple(where))
    return array.at[spots[0]].set(smallest).at[spots[1]].set(high)


def block_levels(stream_key, dims, shards, smallest, top_value):
    loudness = 1.0
    for dim, blocks in shards:
        draws = jax.random.uniform(jax.random.fold_in(jax.random.fold_in(stream_key, 6), dim), (blocks,), jnp.float32, smallest / len(shards), top_value / len(shards))
        loudness = loudness * jnp.repeat(jnp.exp(draws), dims[dim] // blocks).reshape((-1,) + (1,) * (len(dims) - 1 - dim))
    return loudness


def shared_out(key, own, number, rows, number_of, top, reach, slope):
    order = jax.random.permutation(key, number_of)
    heavy_load, usual = shares(number_of, rows * top, reach, slope, True), shares(number_of, rows * top, reach, slope, False)
    places = jnp.arange(number_of)

    def named(tallies, rotation):
        used = int((tallies > 0).sum())
        fixed = max(1, used // 4)
        shifted = fixed + (places - fixed + rotation * (used - fixed)) % max(1, number_of - fixed)
        return jnp.zeros((number_of,), jnp.int32).at[order[jnp.where(places < fixed, places, shifted)]].set(jnp.asarray(tallies, jnp.int32))

    tallies = jnp.where(number % 4 == 0, named(heavy_load, number // 4), named(usual, number - number // 4 - 1))
    mixed = jax.random.permutation(jax.random.fold_in(own, 3), number_of)
    source_of, taker = mixed[0:number_of // 2 * 2:2], mixed[1:number_of // 2 * 2:2]
    margin = jnp.minimum(tallies[source_of] - 1, reach - tallies[taker]) // 2
    margin = jnp.where((source_of == order[0]) | (taker == order[0]) | (tallies[taker] == 0), 0, jnp.maximum(margin, 0))
    shifted = jax.random.randint(jax.random.fold_in(own, 4), (number_of // 2,), 0, 1 << 20) % (margin + 1)
    tallies = tallies.at[source_of].add(-shifted).at[taker].add(shifted)
    members = jnp.searchsorted(jnp.cumsum(tallies), jnp.arange(rows * top), side="right").astype(jnp.int32)
    table = members.reshape(top, rows).T
    table = table[jax.random.permutation(jax.random.fold_in(own, 1), rows)]
    rotation = jax.random.randint(jax.random.fold_in(own, 2), (rows, 1), 0, top)
    return jnp.take_along_axis(table, (jnp.arange(top)[None, :] + rotation) % top, axis=1)


def shares(number_of, total, bound, slope, full):
    weights = [(1 << 20) // math.isqrt(rank ** slope) + 1 for rank in range(1, number_of + 1)]
    largest = bound if full else min(bound, max(-(-total // number_of), total * weights[0] // sum(weights)))
    least = 1 if total - largest >= number_of - 1 else 0
    given, spare = [largest] + [least] * (number_of - 1), total - largest - least * (number_of - 1)
    while spare > 0:
        free = [i for i in range(1, number_of) if given[i] < largest] or [i for i in range(1, number_of) if given[i] < bound]
        whole, remaining = sum([weights[i] for i in free]), spare
        for i in free:
            extra = min(bound - given[i], max(1, remaining * weights[i] // whole), spare)
            given[i] = given[i] + extra
            spare = spare - extra
    return np.array(given)


def normal_values(rng, extent, spread, limit, split=(), kind=jnp.bfloat16):
    factor_of = block_levels(rng, extent, split, -0.22, 0.18) if split else 1.0
    array = jax.random.normal(rng, extent, jnp.float32) * spread * factor_of
    return jnp.minimum(jnp.maximum(array, -limit), limit).astype(kind)


def setup_inputs(seed: int = 0) -> dict:
    streams_of = jax.random.split(jax.random.key(seed), 8)
    queries = normal_values(streams_of[0], (BATCH, LEN, HW), 1.0, 6.0, ((0, 8), (1, 16)))
    d_context = normal_values(streams_of[1], (BATCH, LEN, HW), 2.0, 12.0, ((0, 8), (1, 16)))
    database = normal_values(streams_of[2], (DB_ROWS, NB_LEN, ENC), 1.0, 6.0, ((0, 128),))
    key_weight = normal_values(streams_of[3], (ENC, HW), ENC ** -0.5, 0.1875)
    value_weight = normal_values(streams_of[4], (ENC, HW), ENC ** -0.5, 0.1875)
    neighbour_shard_keys = jax.random.split(jax.random.fold_in(streams_of[5], 1), N_DP * N_SEQ * BLOCKS_DEV // BLOCKS_DEV)
    neighbour_shard_turns = jax.random.permutation(jax.random.fold_in(streams_of[5], 3), N_DP * N_SEQ * BLOCKS_DEV // BLOCKS_DEV)
    neighbour_shard = jax.vmap(lambda own, number: shared_out(jax.random.fold_in(streams_of[5], 2), own, number, BLOCKS_DEV, N_DP, NBR, CAP, 2))(neighbour_shard_keys, neighbour_shard_turns).reshape((N_DP, N_SEQ, BLOCKS_DEV, NBR))
    neighbour_row = with_ends(jax.random.randint(streams_of[6], (N_DP, N_SEQ, BLOCKS_DEV, NBR), 0, ROWS_DEV), jax.random.fold_in(streams_of[6], 1), 0, ROWS_DEV - 1).astype(jnp.int32)
    return dict(queries=queries, d_context=d_context, database=database, key_weight=key_weight, value_weight=value_weight, neighbour_shard=neighbour_shard, neighbour_row=neighbour_row)


def attend(query_block, grad_block, near_rows, key_weight, value_weight):
    score_scale = HD ** -0.5
    key_rows = jnp.dot(near_rows, key_weight, preferred_element_type=jnp.float32).astype(jnp.bfloat16)
    value_rows = jnp.dot(near_rows, value_weight, preferred_element_type=jnp.float32).astype(jnp.bfloat16)
    query_heads = query_block.astype(jnp.float32).reshape(SPAN, HEADS, HD)
    grad_heads = grad_block.astype(jnp.float32).reshape(SPAN, HEADS, HD)
    key_heads = key_rows.astype(jnp.float32).reshape(NBR * NB_LEN, HEADS, HD)
    value_heads = value_rows.astype(jnp.float32).reshape(NBR * NB_LEN, HEADS, HD)
    scores = jnp.einsum('qhd,khd->hqk', query_heads, key_heads) * score_scale
    weights = jnp.exp(scores)
    weights = weights / jnp.sum(weights, axis=-1, keepdims=True)
    weight_half = weights.astype(jnp.bfloat16)
    context_block = jnp.einsum('hqk,khd->qhd', weight_half.astype(jnp.float32), value_heads)
    context_block = context_block.astype(jnp.bfloat16).reshape(SPAN, HW)
    prob_grads = jnp.einsum('qhd,khd->hqk', grad_heads, value_heads)
    row_delta = jnp.sum(weights * prob_grads, axis=-1, keepdims=True)
    score_grads = (score_scale * weights * (prob_grads - row_delta)).astype(jnp.bfloat16)
    query_part = jnp.einsum('hqk,khd->qhd', score_grads.astype(jnp.float32), key_heads)
    query_part = query_part.astype(jnp.bfloat16).reshape(SPAN, HW)
    key_grads = jnp.einsum('hqk,qhd->khd', score_grads.astype(jnp.float32), query_heads)
    key_grads = key_grads.astype(jnp.bfloat16).reshape(NBR * NB_LEN, HW)
    value_grads = jnp.einsum('hqk,qhd->khd', weight_half.astype(jnp.float32), grad_heads)
    value_grads = value_grads.astype(jnp.bfloat16).reshape(NBR * NB_LEN, HW)
    proj_grads = jnp.concatenate([key_grads, value_grads], axis=1)
    both_weights = jnp.concatenate([key_weight, value_weight], axis=1)
    near_grads = jnp.dot(proj_grads, both_weights.T, preferred_element_type=jnp.float32)
    weight_term = jnp.dot(near_rows.T, proj_grads, preferred_element_type=jnp.float32)
    return context_block, query_part, near_grads, weight_term


def reference(queries, d_context, database, key_weight, value_weight, neighbour_shard, neighbour_row):
    lag_rows = SPAN - 1
    block_total = LEN // SPAN
    per_seq = LEN // (SPAN * N_SEQ)
    seq_index = jnp.arange(N_SEQ, dtype=jnp.int32)[None, :, None, None]
    rows = (neighbour_shard * N_SEQ + seq_index) * ROWS_DEV + neighbour_row
    rows = rows.reshape(N_DP, N_SEQ, SEQS_DP, per_seq, NBR).transpose(0, 2, 1, 3, 4)
    rows = rows.reshape(BATCH * block_total, NBR).astype(jnp.int32)
    padding = jnp.zeros((BATCH, lag_rows, HW), jnp.bfloat16)
    shifted_q = jnp.concatenate([queries[:, lag_rows:], padding], axis=1).reshape(BATCH * block_total, SPAN, HW)
    shifted_g = jnp.concatenate([d_context[:, lag_rows:], padding], axis=1).reshape(BATCH * block_total, SPAN, HW)

    def scan_step(accumulated, inputs):
        query_block, grad_block, picked = inputs
        near_rows = jnp.take(database, picked, axis=0).reshape(NBR * NB_LEN, ENC)
        context_block, query_part, near_grads, weight_term = attend(query_block, grad_block, near_rows, key_weight, value_weight)
        return accumulated + weight_term, (context_block, query_part, near_grads)

    start_sum = jnp.zeros((ENC, 2 * HW), jnp.float32)
    accumulated, (context_all, query_all, near_all) = lax.scan(scan_step, start_sum, (shifted_q, shifted_g, rows))
    context_all = context_all.reshape(BATCH, LEN, HW)
    query_all = query_all.reshape(BATCH, LEN, HW)
    context = jnp.concatenate([padding, context_all[:, :LEN - lag_rows]], axis=1)
    query_grad = jnp.concatenate([padding, query_all[:, :LEN - lag_rows]], axis=1)
    database_grad = jnp.zeros((DB_ROWS, NB_LEN, ENC), jnp.float32)
    database_grad = database_grad.at[rows.reshape(-1)].add(near_all.reshape(BATCH * block_total * NBR, NB_LEN, ENC))
    return context, query_grad, database_grad, accumulated[:, :HW], accumulated[:, HW:]
```

```python
import functools

import jax
import jax.numpy as jnp
from jax import lax
from jax.experimental import pallas as pl
from jax.experimental.pallas import tpu as pltpu
from jax.sharding import PartitionSpec as P

HD = 128
SPAN = 64
LAG = SPAN - 1
NB_LEN = 128
CAP = 2
PAD = 8
BF = jnp.bfloat16
F32 = jnp.float32
MESH = pl.DeviceIdType.MESH
VMEM_LIMIT = 60 * 2**20


def dims(n_dp, n_seq):
    side = int(round(n_seq**0.5))
    return n_dp // 2, side


def position():
    dp, seq = lax.axis_index("dp"), lax.axis_index("seq")
    return dp, seq, dp // 2, dp % 2


def toward(nz, rel):
    dp, seq, z, c = position()
    dz, dc = rel // 2, rel % 2
    return (lax.rem(z + dz, nz) * 2 + lax.rem(c + dc, 2), seq)


def back(nz, rel):
    dp, seq, z, c = position()
    dz, dc = rel // 2, rel % 2
    return (lax.rem(z + nz - dz, nz) * 2 + lax.rem(c + dc, 2), seq)


def along(side, first, step):
    dp, seq, z, c = position()
    y, x = seq // side, seq % side
    by_y = (1 - c) if first else c
    ny = lax.rem(y + step * by_y, side)
    nx = lax.rem(x + step * (1 - by_y), side)
    return (dp, ny * side + nx)


def greet(devices):
    barrier = pltpu.get_barrier_semaphore()
    for device in devices:
        pl.semaphore_signal(barrier, inc=1, device_id=device, device_id_type=MESH)
    pl.semaphore_wait(barrier, len(devices))


def remote(src, dst, send, recv, device):
    return pltpu.make_async_remote_copy(
        src_ref=src,
        dst_ref=dst,
        send_sem=send,
        recv_sem=recv,
        device_id=device,
        device_id_type=MESH,
    )


def far_first(nz):
    return sorted(range(2 * nz), key=lambda r: (-min(r // 2, nz - r // 2), r))


def fetch_kernel(
    nz, side,
    req, slot, db, q, g,
    near, arr_out, qs, gs,
    outb, inb, arr, arr_s, heads,
    rq_s, rq_r, ga_s, ga_r, hd_s, hd_r, loc,
):
    n_seq = side * side
    dp, seq, z, c = position()
    before = (dp, lax.rem(seq + n_seq - 1, n_seq))
    after = (dp, lax.rem(seq + 1, n_seq))
    rels = [r for r in far_first(nz) if r]
    greet([toward(nz, r) for r in rels] + [before, after])
    asks = []
    for r in rels:
        copy = remote(req.at[r], arr.at[r], rq_s.at[r], rq_r.at[r], back(nz, r))
        copy.start()
        asks.append(copy)
    arr[0] = req[0]
    head_copies = []
    for t, ref in enumerate((q, g)):
        copy = remote(ref.at[:, 0:SPAN], heads.at[t], hd_s.at[t], hd_r.at[t], before)
        copy.start()
        head_copies.append(copy)
    for copy in asks:
        copy.wait_recv()
    to_smem = pltpu.make_async_copy(arr, arr_s, loc)
    to_smem.start()
    to_smem.wait()
    last_row = db.shape[0] - 1
    sends = []
    for r in rels:
        for k in range(CAP):
            row = jnp.clip(arr_s[r, 0, k], 0, last_row)
            outb[CAP * r + k] = db[row]
        part = pl.ds(CAP * r, CAP)
        copy = remote(outb.at[part], inb.at[part], ga_s.at[r], ga_r.at[r], toward(nz, r))
        copy.start()
        sends.append(copy)
    for k in range(CAP):
        row = jnp.clip(arr_s[0, 0, k], 0, last_row)
        inb[k] = db[row]
    arr_out[...] = arr[...]
    at_end = seq == n_seq - 1
    width = 256
    rows = q.shape[1]
    for t, (ref, out) in enumerate(((q, qs), (g, gs))):
        head_copies[t].wait_recv()
        for j in range(ref.shape[0]):

            def shift(i, carry, ref=ref, out=out, t=t, j=j):
                lanes = pl.ds(pl.multiple_of(i * width, width), width)
                own = ref[j, :, lanes].astype(F32)
                head = heads[t, j, :, lanes].astype(F32)
                head = jnp.where(at_end, jnp.zeros_like(head), head)
                both = jnp.concatenate([own, head], axis=0)
                moved = pltpu.roll(both, rows + SPAN - LAG, 0)[:rows].astype(BF)
                for u in range(rows // SPAN):
                    out[j * (rows // SPAN) + u, :, lanes] = moved[u * SPAN : (u + 1) * SPAN]
                return carry

            lax.fori_loop(0, ref.shape[2] // width, shift, 0)
    for copy in sends:
        copy.wait_recv()
    for i in range(near.shape[0]):
        near[i] = inb[slot[i]]
    for copy in asks + head_copies + sends:
        copy.wait_send()


def nt(a, b):
    return lax.dot_general(a, b, (((1,), (1,)), ((), ())), preferred_element_type=F32)


def tn(a, b):
    return lax.dot_general(a, b, (((0,), (0,)), ((), ())), preferred_element_type=F32)


def nn(a, b):
    return jnp.dot(a, b, preferred_element_type=F32)


def work_kernel(
    nz, side,
    inv, near, qs, gs, kw, vw,
    context, query_grad, returned, wgrad,
    retb, ctx, dq, tails, k2, v2, pg, ng, ngb, near_t, s0, s1, r0, r1, s2, r2, s3, r3,
    own_sem, rt_s, rt_r, tl_s, tl_r, p0_s, p0_r, p1_s, p1_r, p2_s, p2_r, p3_s, p3_r,
):
    n_seq = side * side
    dp, seq, z, c = position()
    y, x = seq // side, seq % side
    before = (dp, lax.rem(seq + n_seq - 1, n_seq))
    after = (dp, lax.rem(seq + 1, n_seq))
    rels = [r for r in far_first(nz) if r]
    steps = range(1, side)
    greet(
        [toward(nz, r) for r in rels]
        + [along(side, True, s) for s in steps]
        + [along(side, False, s) for s in steps]
        + [before, after]
    )
    blocks = qs.shape[0]
    refs = near.shape[0] // NB_LEN
    keys = near.shape[0] // blocks
    enc = near.shape[1]
    pairs = kw.shape[1] // (2 * HD)
    scale = HD**-0.5
    wide = 2 * HD
    first_head = lax.broadcasted_iota(jnp.int32, (SPAN, wide), 1) < HD

    def diagonal(a):
        zero = jnp.zeros_like(a)
        return jnp.concatenate(
            [jnp.where(first_head, a, zero), jnp.where(first_head, zero, a)], axis=0
        )

    def folded(a):
        return jnp.where(first_head, a[:SPAN], a[SPAN:]).astype(BF)

    ng[...] = jnp.zeros_like(ng)

    def pair(hp, carry):
        lanes = pl.ds(pl.multiple_of(hp * wide, wide), wide)
        k_lanes = pl.ds(pl.multiple_of(hp * 2 * wide, 2 * wide), wide)
        v_lanes = pl.ds(pl.multiple_of(hp * 2 * wide + wide, wide), wide)
        k2[...] = nn(near[...], kw[:, lanes]).astype(BF)
        v2[...] = nn(near[...], vw[:, lanes]).astype(BF)
        for b in range(blocks):
            part = slice(b * keys, (b + 1) * keys)
            kb, vb = k2[part], v2[part]
            qd, gd = diagonal(qs[b, :, lanes]), diagonal(gs[b, :, lanes])
            e = jnp.exp(nt(qd, kb) * scale)
            p = e / jnp.sum(e, axis=1, keepdims=True)
            half = p.astype(BF)
            pgr = nt(gd, vb)
            delta = jnp.sum(p * pgr, axis=1, keepdims=True)
            ds = (scale * p * (pgr - delta)).astype(BF)
            ctx[b, :, lanes] = folded(nn(half, vb))
            dq[b, :, lanes] = folded(nn(ds, kb))
            pg[part, k_lanes] = tn(ds, qd).astype(BF)
            pg[part, v_lanes] = tn(half, gd).astype(BF)
        ng[...] += nt(pg[:, k_lanes], kw[:, lanes]) + nt(pg[:, v_lanes], vw[:, lanes])
        return carry

    lax.fori_loop(0, pairs, pair, 0)
    waits = []
    for i in range(refs):
        ngb[i] = ng[i * NB_LEN : (i + 1) * NB_LEN].astype(BF)
    return_copies = []
    for r in rels:
        for k in range(CAP):
            retb[CAP * r + k] = ngb[inv[CAP * r + k]]
        part = pl.ds(CAP * r, CAP)
        copy = remote(retb.at[part], returned.at[part], rt_s.at[r], rt_r.at[r], back(nz, r))
        copy.start()
        return_copies.append(copy)
    for k in range(CAP):
        retb[k] = ngb[inv[k]]
    own_copy = pltpu.make_async_copy(retb.at[pl.ds(0, CAP)], returned.at[pl.ds(0, CAP)], own_sem)
    own_copy.start()
    tail_copies = []
    per_seq = blocks // tails.shape[1]
    for t, ref in enumerate((ctx, dq)):
        for j in range(tails.shape[1]):
            copy = remote(
                ref.at[per_seq * (j + 1) - 1], tails.at[t, j], tl_s.at[t, j], tl_r.at[t, j], after
            )
            copy.start()
            tail_copies.append(copy)
    half_rows = PAD * nz * n_seq
    rows_2 = PAD * nz
    rows_1 = rows_2 * side
    piece = min(128, half_rows)
    per_dev = enc // (2 * nz * n_seq)
    for a in range(2 * half_rows // piece):
        m = lax.broadcasted_iota(jnp.int32, (piece, enc), 0) + a * piece
        core, rest = m // half_rows, m % half_rows
        a1, a2, mz, row = rest // rows_1, (rest // rows_2) % side, (rest // PAD) % nz, rest % PAD
        cell = jnp.where(core == 0, a1 * side + a2, a2 * side + a1)
        column = ((mz * 2 + core) * n_seq + cell) * per_dev + row
        hit = (lax.broadcasted_iota(jnp.int32, (piece, enc), 1) == column) & (row < per_dev)
        pick = jnp.where(hit, 1.0, 0.0).astype(BF)
        near_t[a * piece : (a + 1) * piece] = nt(pick, near[...]).astype(BF)
    chunks = s0.shape[0]
    cw = s0.shape[3]
    sibling = (z * 2 + (1 - c), seq)
    my1 = jnp.where(c == 0, y, x)
    my2 = jnp.where(c == 0, x, y)
    phase0, phase1, phase2, phase3 = [], [], [], []

    def product(core, i):
        rows = pl.ds(pl.multiple_of(core * half_rows, half_rows), half_rows)
        out = nn(near_t[rows], pg[:, i * cw : (i + 1) * cw])
        return out.astype(BF).reshape(side, rows_1, cw)

    def send_first(i):
        phase0[i].wait_recv()
        s1[i] = (s1[i].astype(F32) + r0[i].astype(F32)).astype(BF)
        out = []
        for s in steps:
            to = lax.rem(my1 + s, side)
            copy = remote(
                s1.at[i, to], r1.at[i, s - 1], p1_s.at[i, s - 1], p1_r.at[i, s - 1],
                along(side, True, s),
            )
            copy.start()
            out.append(copy)
        phase1.append(out)

    for i in range(chunks):
        s0[i] = product(1 - c, i)
        copy = remote(s0.at[i], r0.at[i], p0_s.at[i], p0_r.at[i], sibling)
        copy.start()
        phase0.append(copy)
        s1[i] = product(c, i)
        if i:
            send_first(i - 1)
    send_first(chunks - 1)
    at_start = seq == 0
    width = 256
    rows = per_seq * SPAN
    for t, (ref, out) in enumerate(((ctx, context), (dq, query_grad))):
        for j in range(tails.shape[1]):
            tail_copies[t * tails.shape[1] + j].wait_recv()

            def shift(i, carry, ref=ref, out=out, t=t, j=j):
                lanes = pl.ds(pl.multiple_of(i * width, width), width)
                tail = tails[t, j, :, lanes].astype(F32)
                tail = jnp.where(at_start, jnp.zeros_like(tail), tail)
                own = [ref[per_seq * j + u, :, lanes].astype(F32) for u in range(per_seq)]
                both = jnp.concatenate([tail] + own, axis=0)
                out[j, :, lanes] = pltpu.roll(both, rows + LAG, 0)[:rows].astype(BF)
                return carry

            lax.fori_loop(0, ref.shape[2] // width, shift, 0)
    for i in range(chunks):
        total = s1[i, my1].astype(F32)
        for s in steps:
            phase1[i][s - 1].wait_recv()
            total = total + r1[i, s - 1].astype(F32)
        s2[i] = total.astype(BF).reshape(side, rows_2, cw)
        out = []
        for s in steps:
            to = lax.rem(my2 + s, side)
            copy = remote(
                s2.at[i, to], r2.at[i, s - 1], p2_s.at[i, s - 1], p2_r.at[i, s - 1],
                along(side, False, s),
            )
            copy.start()
            out.append(copy)
        phase2.append(out)
    for i in range(chunks):
        total = s2[i, my2].astype(F32)
        for s in steps:
            phase2[i][s - 1].wait_recv()
            total = total + r2[i, s - 1].astype(F32)
        keys_part = [total[:, a : a + wide] for a in range(0, cw, 2 * wide)]
        values_part = [total[:, a + wide : a + 2 * wide] for a in range(0, cw, 2 * wide)]
        for part in range(nz):
            row = slice(part * PAD, (part + 1) * PAD)
            for a in range(cw // (2 * wide)):
                both = jnp.concatenate([keys_part[a][row], values_part[a][row]], axis=0)
                at = i * cw // 2 + a * wide
                s3[part, :, at : at + wide] = both.astype(BF)
    for s in range(1, nz):
        copy = remote(
            s3.at[lax.rem(z + s, nz)], r3.at[s - 1], p3_s.at[s - 1], p3_r.at[s - 1],
            (lax.rem(z + s, nz) * 2 + c, seq),
        )
        copy.start()
        phase3.append(copy)
    total = s3[z].astype(F32)
    for s in range(1, nz):
        phase3[s - 1].wait_recv()
        total = total + r3[s - 1].astype(F32)
    wgrad[...] = total
    own_copy.wait()
    for copy in return_copies:
        copy.wait_recv()
    for copy in (
        return_copies + tail_copies + phase0 + sum(phase1, []) + sum(phase2, []) + phase3
    ):
        copy.wait_send()


def scatter_kernel(arrived, returned, out):
    out[...] = jnp.zeros_like(out)
    for s in range(returned.shape[0]):
        row = arrived[s]
        part = returned[s].astype(F32)
        out[jnp.maximum(row, 0)] += jnp.where(row >= 0, part, jnp.zeros_like(part))


def local(n_dp, n_seq, queries, d_context, database, key_weight, value_weight, shard, wanted):
    nz, side = dims(n_dp, n_seq)
    seqs, span, width = queries.shape
    blocks = seqs * span // SPAN
    refs = blocks * shard.shape[-1]
    slots = n_dp * CAP
    enc = database.shape[2]
    dp = lax.axis_index("dp")
    target, wanted = shard.reshape(refs), wanted.reshape(refs)
    order = jnp.arange(refs, dtype=jnp.int32)
    earlier = (target[:, None] == target[None, :]) & (order[None, :] < order[:, None])
    rank = jnp.sum(earlier.astype(jnp.int32), axis=1)
    rel = ((dp // 2 - target // 2 + nz) % nz) * 2 + (dp + target) % 2
    slot = rel * CAP + rank
    placed = slot[:, None] == jnp.arange(slots, dtype=jnp.int32)[None, :]
    request = jnp.sum(jnp.where(placed, wanted[:, None] + 1, 0), axis=0) - 1
    source = jnp.sum(jnp.where(placed, order[:, None], 0), axis=0)
    request = jnp.pad(request.reshape(n_dp, 1, CAP), ((0, 0), (0, 7), (0, 126)))
    vmem = pl.BlockSpec(memory_space=pltpu.VMEM)
    smem = pl.BlockSpec(memory_space=pltpu.SMEM)
    anywhere = pl.BlockSpec(memory_space=pl.ANY)
    dma = pltpu.SemaphoreType.DMA
    near, arrived, shifted_q, shifted_g = pl.pallas_call(
        functools.partial(fetch_kernel, nz, side),
        name="fetch",
        out_shape=(
            jax.ShapeDtypeStruct((refs, NB_LEN, enc), BF),
            jax.ShapeDtypeStruct((n_dp, 8, 128), jnp.int32),
            jax.ShapeDtypeStruct((blocks, SPAN, width), BF),
            jax.ShapeDtypeStruct((blocks, SPAN, width), BF),
        ),
        in_specs=[vmem, smem, vmem, vmem, vmem],
        out_specs=(vmem, vmem, vmem, vmem),
        scratch_shapes=[
            pltpu.VMEM((slots, NB_LEN, enc), BF),
            pltpu.VMEM((slots, NB_LEN, enc), BF),
            pltpu.VMEM((n_dp, 8, 128), jnp.int32),
            pltpu.SMEM((n_dp, 8, 128), jnp.int32),
            pltpu.VMEM((2, seqs, SPAN, width), BF),
            dma((n_dp,)),
            dma((n_dp,)),
            dma((n_dp,)),
            dma((n_dp,)),
            dma((2,)),
            dma((2,)),
            dma,
        ],
        compiler_params=pltpu.CompilerParams(
            collective_id=0, has_side_effects=True, vmem_limit_bytes=VMEM_LIMIT
        ),
    )(request, slot, database, queries, d_context)
    half_rows = PAD * nz * n_seq
    rows_2 = PAD * nz
    rows_1 = rows_2 * side
    chunk = 4 * 2 * HD
    chunks = 2 * width // chunk
    more = side - 1
    context, query_grad, returned, wgrad = pl.pallas_call(
        functools.partial(work_kernel, nz, side),
        name="work",
        out_shape=(
            jax.ShapeDtypeStruct((seqs, span, width), BF),
            jax.ShapeDtypeStruct((seqs, span, width), BF),
            jax.ShapeDtypeStruct((slots, NB_LEN, enc), BF),
            jax.ShapeDtypeStruct((2 * PAD, width), F32),
        ),
        in_specs=[smem, vmem, vmem, vmem, vmem, vmem],
        out_specs=(vmem, vmem, anywhere, vmem),
        scratch_shapes=[
            pltpu.VMEM((slots, NB_LEN, enc), BF),
            pltpu.VMEM((blocks, SPAN, width), BF),
            pltpu.VMEM((blocks, SPAN, width), BF),
            pltpu.VMEM((2, seqs, SPAN, width), BF),
            pltpu.VMEM((refs * NB_LEN, 2 * HD), BF),
            pltpu.VMEM((refs * NB_LEN, 2 * HD), BF),
            pltpu.VMEM((refs * NB_LEN, 2 * width), BF),
            pltpu.VMEM((refs * NB_LEN, enc), F32),
            pltpu.VMEM((refs, NB_LEN, enc), BF),
            pltpu.VMEM((2 * half_rows, refs * NB_LEN), BF),
            pltpu.VMEM((chunks, side, rows_1, chunk), BF),
            pltpu.VMEM((chunks, side, rows_1, chunk), BF),
            pltpu.VMEM((chunks, side, rows_1, chunk), BF),
            pltpu.VMEM((chunks, more, rows_1, chunk), BF),
            pltpu.VMEM((chunks, side, rows_2, chunk), BF),
            pltpu.VMEM((chunks, more, rows_2, chunk), BF),
            pltpu.VMEM((nz, 2 * PAD, width), BF),
            pltpu.VMEM((nz - 1, 2 * PAD, width), BF),
            dma,
            dma((n_dp,)),
            dma((n_dp,)),
            dma((2, seqs)),
            dma((2, seqs)),
            dma((chunks,)),
            dma((chunks,)),
            dma((chunks, more)),
            dma((chunks, more)),
            dma((chunks, more)),
            dma((chunks, more)),
            dma((nz - 1,)),
            dma((nz - 1,)),
        ],
        compiler_params=pltpu.CompilerParams(
            collective_id=1, has_side_effects=True, vmem_limit_bytes=VMEM_LIMIT
        ),
    )(
        source,
        near.reshape(refs * NB_LEN, enc),
        shifted_q,
        shifted_g,
        key_weight,
        value_weight,
    )
    rows = 16
    database_grad = pl.pallas_call(
        scatter_kernel,
        name="scatter",
        out_shape=jax.ShapeDtypeStruct(database.shape, F32),
        grid_spec=pltpu.PrefetchScalarGridSpec(
            num_scalar_prefetch=1,
            grid=(NB_LEN // rows,),
            in_specs=[pl.BlockSpec((slots, rows, enc), lambda i, s: (0, i, 0))],
            out_specs=pl.BlockSpec((database.shape[0], rows, enc), lambda i, s: (0, i, 0)),
        ),
    )(arrived[:, 0, :CAP].reshape(slots), returned)
    per_dev = enc // (n_dp * n_seq)
    return (
        context,
        query_grad,
        database_grad,
        wgrad[:per_dev],
        wgrad[PAD : PAD + per_dev],
    )


def solution(mesh):
    return jax.shard_map(
        functools.partial(local, mesh.shape["dp"], mesh.shape["seq"]),
        mesh=mesh,
        in_specs=(
            P("dp", "seq", None),
            P("dp", "seq", None),
            P(("dp", "seq"), None, None),
            P(),
            P(),
            P("dp", "seq", None, None),
            P("dp", "seq", None, None),
        ),
        out_specs=(
            P("dp", "seq", None),
            P("dp", "seq", None),
            P(("dp", "seq"), None, None),
            P(("dp", "seq"), None),
            P(("dp", "seq"), None),
        ),
        check_vma=False,
    )
```

```python
import functools

import jax
import jax.numpy as jnp
from jax import lax
from jax.experimental import pallas as pl
from jax.experimental.pallas import tpu as pltpu
from jax.sharding import PartitionSpec as P

HD = 128
SPAN = 64
LAG = SPAN - 1
NB_LEN = 128
CAP = 2
PAD = 8
BF = jnp.bfloat16
F32 = jnp.float32
MESH = pl.DeviceIdType.MESH
VMEM_LIMIT = 62 * 2**20


def dims(n_dp, n_seq):
    side = int(round(n_seq**0.5))
    return n_dp // 2, side


def position():
    dp, seq = lax.axis_index("dp"), lax.axis_index("seq")
    return dp, seq, dp // 2, dp % 2


def toward(nz, rel):
    dp, seq, z, c = position()
    dz, dc = rel // 2, rel % 2
    return (lax.rem(z + dz, nz) * 2 + lax.rem(c + dc, 2), seq)


def back(nz, rel):
    dp, seq, z, c = position()
    dz, dc = rel // 2, rel % 2
    return (lax.rem(z + nz - dz, nz) * 2 + lax.rem(c + dc, 2), seq)


def along(side, first, step):
    dp, seq, z, c = position()
    y, x = seq // side, seq % side
    by_y = (1 - c) if first else c
    ny = lax.rem(y + step * by_y, side)
    nx = lax.rem(x + step * (1 - by_y), side)
    return (dp, ny * side + nx)


def greet(devices):
    barrier = pltpu.get_barrier_semaphore()
    for device in devices:
        pl.semaphore_signal(barrier, inc=1, device_id=device, device_id_type=MESH)
    pl.semaphore_wait(barrier, len(devices))


def remote(src, dst, send, recv, device):
    return pltpu.make_async_remote_copy(
        src_ref=src,
        dst_ref=dst,
        send_sem=send,
        recv_sem=recv,
        device_id=device,
        device_id_type=MESH,
    )


def far_first(nz):
    return sorted(range(2 * nz), key=lambda r: (-min(r // 2, nz - r // 2), r))


def nt(a, b):
    return lax.dot_general(a, b, (((1,), (1,)), ((), ())), preferred_element_type=F32)


def tn(a, b):
    return lax.dot_general(a, b, (((0,), (0,)), ((), ())), preferred_element_type=F32)


def nn(a, b):
    return jnp.dot(a, b, preferred_element_type=F32)


def main_kernel(
    nz, side,
    named, db_hbm, q_hbm, g_hbm, kw_hbm, vw_hbm,
    context, query_grad, returned, arrived, wgrad,
    db, outb, inb, req, arr, arr_s, heads, q, g, qs, gs, kw, vw, kv, pg, ng, sa_k, sa_v, sb_k, sb_v, tails,
    r2, s3, r3,
    ld, rq_s, rq_r, ga_s, ga_r, hd_s, hd_r, own_sem, rt_s, rt_r, tl_s, tl_r,
    p0_s, p0_r, p1_s, p1_r, p2_s, p2_r, p3_s, p3_r, free0, free1,
):
    n_seq = side * side
    dp, seq, z, c = position()
    y, x = seq // side, seq % side
    before = (dp, lax.rem(seq + n_seq - 1, n_seq))
    after = (dp, lax.rem(seq + 1, n_seq))
    sibling = (z * 2 + (1 - c), seq)
    rels = [r for r in far_first(nz) if r]
    steps = range(1, side)
    loads = []
    pairs_in = ((db_hbm, db), (kw_hbm, kw), (vw_hbm, vw), (q_hbm, q), (g_hbm, g))
    for i, (src, dst) in enumerate(pairs_in):
        copy = pltpu.make_async_copy(src, dst, ld.at[i])
        copy.start()
        loads.append(copy)
    picks, blocks = named.shape[2], named.shape[3]
    refs = blocks * picks
    slots = CAP * 2 * nz
    held = db_hbm.shape[0]
    both = [named[0, 0, i % picks, i // picks] for i in range(refs)]
    target, row_of = [a // held for a in both], [a % held for a in both]
    slot = []
    for i in range(refs):
        rank = sum([jnp.where(target[j] == target[i], 1, 0) for j in range(i)], jnp.int32(0))
        dz = lax.rem(z + nz - target[i] // 2, nz)
        dc = lax.rem(c + target[i], 2)
        slot.append((dz * 2 + dc) * CAP + jnp.minimum(rank, CAP - 1))
    lane = lax.broadcasted_iota(jnp.int32, (8, 128), 1)
    source = []
    for r in range(2 * nz):
        tile = jnp.zeros((8, 128), jnp.int32)
        for k in range(CAP):
            here = [slot[i] == CAP * r + k for i in range(refs)]
            asked = sum([jnp.where(here[i], row_of[i] + 1, 0) for i in range(refs)], jnp.int32(0))
            mine = sum([jnp.where(here[i], i, 0) for i in range(refs)], jnp.int32(0))
            source.append(jnp.minimum(mine, refs - 1))
            tile = jnp.where(lane == k, asked - 1, tile)
        req[r] = tile
    greet(
        [toward(nz, r) for r in rels]
        + [along(side, True, s) for s in steps]
        + [along(side, False, s) for s in steps]
        + [before, after]
    )
    asks = []
    for r in rels:
        copy = remote(req.at[r], arr.at[r], rq_s.at[r], rq_r.at[r], back(nz, r))
        copy.start()
        asks.append(copy)
    arr[0] = req[0]
    head_copies = []
    for t, ref in enumerate((q_hbm, g_hbm)):
        copy = remote(ref.at[:, 0:SPAN], heads.at[t], hd_s.at[t], hd_r.at[t], before)
        copy.start()
        head_copies.append(copy)
    for copy in asks:
        copy.wait_recv()
    to_smem = pltpu.make_async_copy(arr, arr_s, ld.at[5])
    to_smem.start()
    loads[0].wait()
    to_smem.wait()
    last_row = db.shape[0] - 1
    sends = {}
    for r in rels:
        for k in range(CAP):
            row = jnp.clip(arr_s[r, 0, k], 0, last_row)
            outb[CAP * r + k] = db[row]
        part = pl.ds(CAP * r, CAP)
        copy = remote(outb.at[part], inb.at[part], ga_s.at[r], ga_r.at[r], toward(nz, r))
        copy.start()
        sends[r] = copy
    for k in range(CAP):
        row = jnp.clip(arr_s[0, 0, k], 0, last_row)
        inb[k] = db[row]
    for r in range(2 * nz):
        for k in range(CAP):
            arrived[CAP * r + k] = arr_s[r, 0, k]
    enc = db.shape[2]
    half_rows = PAD * nz * n_seq
    rows_2 = PAD * nz
    rows_1 = rows_2 * side
    piece = NB_LEN
    per_dev = enc // (2 * nz * n_seq)
    pieces = 2 * half_rows // piece
    for a in range(pieces):
        m = lax.broadcasted_iota(jnp.int32, (piece, 128), 0) + a * piece
        core, rest = m // half_rows, m % half_rows
        a1, a2, mz, row = rest // rows_1, (rest // rows_2) % side, (rest // PAD) % nz, rest % PAD
        cell = jnp.where(core == 0, a1 * side + a2, a2 * side + a1)
        column = ((mz * 2 + core) * n_seq + cell) * per_dev + row
        column = jnp.where(row < per_dev, column, enc)
        for o in range(0, enc, 128):
            hit = lax.broadcasted_iota(jnp.int32, (piece, 128), 1) + o == column
            db[a, :, o : o + 128] = jnp.where(hit, 1.0, 0.0).astype(BF)
    at_end = seq == n_seq - 1
    width = 256
    seqs, rows = q.shape[0], q.shape[1]
    per_seq = rows // SPAN
    for t, (ref, out) in enumerate(((q, qs), (g, gs))):
        loads[3 + t].wait()
        head_copies[t].wait_recv()
        for j in range(seqs):

            def shift(i, carry, ref=ref, out=out, t=t, j=j):
                lanes = pl.ds(pl.multiple_of(i * width, width), width)
                own = ref[j, :, lanes].astype(F32)
                head = heads[t, j, :, lanes].astype(F32)
                head = jnp.where(at_end, jnp.zeros_like(head), head)
                both = jnp.concatenate([own, head], axis=0)
                moved = pltpu.roll(both, rows + SPAN - LAG, 0)[:rows].astype(BF)
                for u in range(per_seq):
                    out[j * per_seq + u, :, lanes] = moved[u * SPAN : (u + 1) * SPAN]
                return carry

            lax.fori_loop(0, ref.shape[2] // width, shift, 0)
    hw = kw.shape[1]
    loads[1].wait()
    loads[2].wait()
    step_lanes = 512
    for r in [0, 1] + [r for r in rels if r != 1]:
        if r:
            sends[r].wait_recv()

        def project(i, carry, r=r):
            lanes = pl.ds(pl.multiple_of(i * step_lanes, step_lanes), step_lanes)
            later = pl.ds(pl.multiple_of(hw + i * step_lanes, step_lanes), step_lanes)
            rows_in = inb[CAP * r : CAP * (r + 1)].reshape(CAP * NB_LEN, enc)
            keys = nn(rows_in, kw[:, lanes]).astype(BF)
            kv[CAP * r : CAP * (r + 1), :, lanes] = keys.reshape(CAP, NB_LEN, step_lanes)
            values = nn(rows_in, vw[:, lanes]).astype(BF)
            kv[CAP * r : CAP * (r + 1), :, later] = values.reshape(CAP, NB_LEN, step_lanes)
            return carry

        lax.fori_loop(0, hw // step_lanes, project, 0)
    scale = HD**-0.5
    wide = 2 * HD
    first_head = lax.broadcasted_iota(jnp.int32, (SPAN, wide), 1) < HD

    def diagonal(a):
        zero = jnp.zeros_like(a)
        return jnp.concatenate(
            [jnp.where(first_head, a, zero), jnp.where(first_head, zero, a)], axis=0
        )

    def folded(a):
        return jnp.where(first_head, a[:SPAN], a[SPAN:]).astype(BF)

    def attend(hp, stage_k, stage_v, beside):
        lanes = pl.ds(pl.multiple_of(hp * wide, wide), wide)
        later = pl.ds(pl.multiple_of(hw + hp * wide, wide), wide)
        every = range(blocks)
        kb, vb, qd, gd = [], [], [], []
        for b in every:
            mine = [slot[picks * b + i] for i in range(picks)]
            kb.append(jnp.concatenate([kv[i, :, lanes] for i in mine], axis=0))
            vb.append(jnp.concatenate([kv[i, :, later] for i in mine], axis=0))
            qd.append(diagonal(qs[b, :, lanes]))
            gd.append(diagonal(gs[b, :, lanes]))
        scores = [nt(qd[b], kb[b]) for b in every]
        pgr = [nt(gd[b], vb[b]) for b in every]
        beside(0)
        p = []
        for b in every:
            e = jnp.exp(scores[b] * scale)
            p.append(e / jnp.sum(e, axis=1, keepdims=True))
        half = [p[b].astype(BF) for b in every]
        beside(1)
        out = [folded(nn(half[b], vb[b])) for b in every]
        value_g = [tn(half[b], gd[b]).astype(BF) for b in every]
        beside(2)
        ds = []
        for b in every:
            delta = jnp.sum(p[b] * pgr[b], axis=1, keepdims=True)
            ds.append((scale * p[b] * (pgr[b] - delta)).astype(BF))
        beside(3)
        back_out = [folded(nn(ds[b], kb[b])) for b in every]
        key_g = [tn(ds[b], qd[b]).astype(BF) for b in every]
        for b in every:
            rows_b = slice(b * picks * NB_LEN, (b + 1) * picks * NB_LEN)
            qs[b, :, lanes] = out[b]
            gs[b, :, lanes] = back_out[b]
            stage_k[rows_b] = key_g[b]
            stage_v[rows_b] = value_g[b]
            pg[picks * b : picks * (b + 1), :, lanes] = key_g[b].reshape(picks, NB_LEN, wide)
            pg[picks * b : picks * (b + 1), :, later] = value_g[b].reshape(picks, NB_LEN, wide)

    def add_near(hp, stage_k, stage_v):
        lanes = pl.ds(pl.multiple_of(hp * wide, wide), wide)

        def add(b):
            rows_b = slice(b * picks * NB_LEN, (b + 1) * picks * NB_LEN)
            ng[rows_b] += nt(stage_k[rows_b], kw[:, lanes]) + nt(stage_v[rows_b], vw[:, lanes])

        return add

    ng[...] = jnp.zeros_like(ng)
    sb_k[...] = jnp.zeros_like(sb_k)
    sb_v[...] = jnp.zeros_like(sb_v)

    def two_pairs(i, carry):
        attend(2 * i, sa_k, sa_v, add_near(jnp.maximum(2 * i - 1, 0), sb_k, sb_v))
        attend(2 * i + 1, sb_k, sb_v, add_near(2 * i, sa_k, sa_v))
        return carry

    lax.fori_loop(0, hw // (2 * wide), two_pairs, 0)
    last = add_near(hw // wide - 1, sb_k, sb_v)
    for b in range(blocks):
        last(b)
    for i in range(refs):
        db[pieces + i] = ng[i * NB_LEN : (i + 1) * NB_LEN].astype(BF)
    pl.semaphore_signal(free0, inc=1, device_id=sibling, device_id_type=MESH)
    for s in steps:
        pl.semaphore_signal(free1, inc=1, device_id=along(side, True, s), device_id_type=MESH)
    for copy in sends.values():
        copy.wait_send()
    return_copies = []

    def give_back(r):
        for k in range(CAP):
            outb[CAP * r + k] = db[pieces + source[CAP * r + k]]
        part = pl.ds(CAP * r, CAP)
        if r:
            copy = remote(outb.at[part], returned.at[part], rt_s.at[r], rt_r.at[r], back(nz, r))
            return_copies.append(copy)
        else:
            copy = pltpu.make_async_copy(outb.at[part], returned.at[part], own_sem)
            own_copies.append(copy)
        copy.start()

    own_copies = []
    chunks = p0_s.shape[0]
    cw = 2 * hw // chunks
    my1 = jnp.where(c == 0, y, x)
    my2 = jnp.where(c == 0, x, y)
    phase0, phase1, phase2, phase3 = [], [], [], []

    def rows_of(a):
        return pl.ds(pl.multiple_of(a * rows_2, rows_2), rows_2)

    def lanes_of(a):
        return pl.ds(pl.multiple_of(a * cw, cw), cw)

    def product(core, i, base):
        start = pl.multiple_of(core * half_rows, half_rows)
        some = jnp.concatenate([part[pl.ds(start, half_rows)] for part in near_t], axis=1)
        for o in range(0, cw, step_lanes):
            these = pg[:, :, i * cw + o : i * cw + o + step_lanes]
            out = nn(some, these.reshape(refs * NB_LEN, step_lanes)).astype(BF)
            for a in range(side):
                kv[base + i, :, a * cw + o : a * cw + o + step_lanes] = out[
                    a * rows_1 : (a + 1) * rows_1
                ]

    def multiply(i):
        product(1 - c, i, 0)
        if i == 0:
            pl.semaphore_wait(free0, 1)
        copy = remote(kv.at[i], kv.at[2 * chunks + i], p0_s.at[i], p0_r.at[i], sibling)
        copy.start()
        phase0.append(copy)
        product(c, i, chunks)

    def send_first(i):
        phase0[i].wait_recv()
        kv[chunks + i] = (kv[chunks + i].astype(F32) + kv[2 * chunks + i].astype(F32)).astype(BF)
        if i == 0:
            pl.semaphore_wait(free1, side - 1)
        out = []
        for s in steps:
            to = lax.rem(my1 + s, side)
            copy = remote(
                kv.at[chunks + i, :, lanes_of(to)],
                kv.at[3 * chunks + i, :, pl.ds((s - 1) * cw, cw)],
                p1_s.at[i, s - 1], p1_r.at[i, s - 1], along(side, True, s),
            )
            copy.start()
            out.append(copy)
        phase1.append(out)

    for r in rels + [0]:
        give_back(r)
    tail_copies = []
    for t, ref in enumerate((qs, gs)):
        for j in range(seqs):
            copy = remote(
                ref.at[per_seq * (j + 1) - 1], tails.at[t, j], tl_s.at[t, j], tl_r.at[t, j], after
            )
            copy.start()
            tail_copies.append(copy)
    near_t = (sa_k, sa_v, sb_k, sb_v)
    for i in range(0, refs, 2):
        both = jnp.concatenate([inb[slot[i]], inb[slot[i + 1]]], axis=0)
        near_t[i // 2][...] = nt(db[0:pieces].reshape(2 * half_rows, enc), both).astype(BF)
    for i in range(chunks + 1):
        if i < chunks:
            multiply(i)
        if i:
            send_first(i - 1)
    at_start = seq == 0
    outs = []
    for t, (ref, out, hbm) in enumerate(((qs, q, context), (gs, g, query_grad))):
        for j in range(seqs):
            tail_copies[t * seqs + j].wait_recv()

            def unshift(i, carry, ref=ref, out=out, t=t, j=j):
                lanes = pl.ds(pl.multiple_of(i * width, width), width)
                tail = tails[t, j, :, lanes].astype(F32)
                tail = jnp.where(at_start, jnp.zeros_like(tail), tail)
                own = [ref[per_seq * j + u, :, lanes].astype(F32) for u in range(per_seq)]
                both = jnp.concatenate([tail] + own, axis=0)
                out[j, :, lanes] = pltpu.roll(both, rows + LAG, 0)[:rows].astype(BF)
                return carry

            lax.fori_loop(0, ref.shape[2] // width, unshift, 0)
        copy = pltpu.make_async_copy(out, hbm, ld.at[6 + t])
        copy.start()
        outs.append(copy)
    for i in range(chunks):
        total = kv[chunks + i, :, lanes_of(my1)].astype(F32)
        for s in steps:
            phase1[i][s - 1].wait_recv()
            total = total + kv[3 * chunks + i, :, (s - 1) * cw : s * cw].astype(F32)
        kv[3 * chunks + i, :, (side - 1) * cw : side * cw] = total.astype(BF)
        out = []
        for s in steps:
            to = lax.rem(my2 + s, side)
            copy = remote(
                kv.at[3 * chunks + i, rows_of(to), pl.ds((side - 1) * cw, cw)], r2.at[i, s - 1], p2_s.at[i, s - 1], p2_r.at[i, s - 1],
                along(side, False, s),
            )
            copy.start()
            out.append(copy)
        phase2.append(out)
    totals = []
    for i in range(chunks):
        total = kv[3 * chunks + i, rows_of(my2), (side - 1) * cw : side * cw].astype(F32)
        for s in steps:
            phase2[i][s - 1].wait_recv()
            total = total + r2[i, s - 1].astype(F32)
        totals.append(total)
        if i >= chunks // 2:
            a = i - chunks // 2
            for part in range(nz):
                row = slice(part * PAD, (part + 1) * PAD)
                both = jnp.concatenate([totals[a][row], total[row]], axis=0)
                s3[part, :, a * cw : (a + 1) * cw] = both.astype(BF)
    for s in range(1, nz):
        copy = remote(
            s3.at[lax.rem(z + s, nz)], r3.at[s - 1], p3_s.at[s - 1], p3_r.at[s - 1],
            (lax.rem(z + s, nz) * 2 + c, seq),
        )
        copy.start()
        phase3.append(copy)
    total = s3[z].astype(F32)
    for s in range(1, nz):
        phase3[s - 1].wait_recv()
        total = total + r3[s - 1].astype(F32)
    wgrad[...] = total
    for copy in outs + own_copies:
        copy.wait()
    for copy in return_copies:
        copy.wait_recv()
    for copy in (
        asks + head_copies + return_copies + tail_copies + phase0
        + sum(phase1, []) + sum(phase2, []) + phase3
    ):
        copy.wait_send()


def finish_kernel(arrived, returned, wgrad, out, key_part, value_part):
    @pl.when(pl.program_id(0) == 0)
    def _():
        per_dev = key_part.shape[0]
        key_part[...] = wgrad[0:per_dev]
        value_part[...] = wgrad[PAD : PAD + per_dev]

    out[...] = jnp.zeros_like(out)
    for s in range(returned.shape[0]):
        row = arrived[s]
        part = returned[s].astype(F32)
        out[jnp.clip(row, 0, out.shape[0] - 1)] += jnp.where(row >= 0, part, jnp.zeros_like(part))


def local(n_dp, n_seq, queries, d_context, database, key_weight, value_weight, shard, wanted):
    nz, side = dims(n_dp, n_seq)
    seqs, span, width = queries.shape
    blocks = seqs * span // SPAN
    refs = blocks * shard.shape[-1]
    slots = n_dp * CAP
    enc = database.shape[2]
    vmem = pl.BlockSpec(memory_space=pltpu.VMEM)
    smem = pl.BlockSpec(memory_space=pltpu.SMEM)
    anywhere = pl.BlockSpec(memory_space=pl.ANY)
    dma = pltpu.SemaphoreType.DMA
    regular = pltpu.SemaphoreType.REGULAR
    rows_2 = PAD * nz
    chunks = 4
    chunk = 2 * width // chunks
    more = side - 1
    context, query_grad, returned, arrived, wgrad = pl.pallas_call(
        functools.partial(main_kernel, nz, side),
        name="main",
        out_shape=(
            jax.ShapeDtypeStruct((seqs, span, width), BF),
            jax.ShapeDtypeStruct((seqs, span, width), BF),
            jax.ShapeDtypeStruct((slots, NB_LEN, enc), BF),
            jax.ShapeDtypeStruct((slots,), jnp.int32),
            jax.ShapeDtypeStruct((2 * PAD, width), F32),
        ),
        in_specs=[smem] + [anywhere] * 5,
        out_specs=(anywhere, anywhere, anywhere, smem, vmem),
        scratch_shapes=[
            pltpu.VMEM((database.shape[0], NB_LEN, enc), BF),
            pltpu.VMEM((slots, NB_LEN, enc), BF),
            pltpu.VMEM((slots, NB_LEN, enc), BF),
            pltpu.VMEM((n_dp, 8, 128), jnp.int32),
            pltpu.VMEM((n_dp, 8, 128), jnp.int32),
            pltpu.SMEM((n_dp, 8, 128), jnp.int32),
            pltpu.VMEM((2, seqs, SPAN, width), BF),
            pltpu.VMEM((seqs, span, width), BF),
            pltpu.VMEM((seqs, span, width), BF),
            pltpu.VMEM((blocks, SPAN, width), BF),
            pltpu.VMEM((blocks, SPAN, width), BF),
            pltpu.VMEM((enc, width), BF),
            pltpu.VMEM((enc, width), BF),
            pltpu.VMEM((slots, NB_LEN, 2 * width), BF),
            pltpu.VMEM((refs, NB_LEN, 2 * width), BF),
            pltpu.VMEM((refs * NB_LEN, enc), F32),
            pltpu.VMEM((refs * NB_LEN, 2 * HD), BF),
            pltpu.VMEM((refs * NB_LEN, 2 * HD), BF),
            pltpu.VMEM((refs * NB_LEN, 2 * HD), BF),
            pltpu.VMEM((refs * NB_LEN, 2 * HD), BF),
            pltpu.VMEM((2, seqs, SPAN, width), BF),
            pltpu.VMEM((chunks, more, rows_2, chunk), BF),
            pltpu.VMEM((nz, 2 * PAD, width), BF),
            pltpu.VMEM((nz - 1, 2 * PAD, width), BF),
            dma((8,)),
            dma((n_dp,)),
            dma((n_dp,)),
            dma((n_dp,)),
            dma((n_dp,)),
            dma((2,)),
            dma((2,)),
            dma,
            dma((n_dp,)),
            dma((n_dp,)),
            dma((2, seqs)),
            dma((2, seqs)),
            dma((chunks,)),
            dma((chunks,)),
            dma((chunks, more)),
            dma((chunks, more)),
            dma((chunks, more)),
            dma((chunks, more)),
            dma((nz - 1,)),
            dma((nz - 1,)),
            regular,
            regular,
        ],
        compiler_params=pltpu.CompilerParams(
            collective_id=0, has_side_effects=True, vmem_limit_bytes=VMEM_LIMIT
        ),
    )((shard * database.shape[0] + wanted).swapaxes(2, 3), database, queries, d_context, key_weight, value_weight)
    rows = 32
    per_dev = enc // (n_dp * n_seq)
    part = jax.ShapeDtypeStruct((per_dev, width), F32)
    database_grad, key_part, value_part = pl.pallas_call(
        finish_kernel,
        name="finish",
        out_shape=(jax.ShapeDtypeStruct(database.shape, F32), part, part),
        grid_spec=pltpu.PrefetchScalarGridSpec(
            num_scalar_prefetch=1,
            grid=(NB_LEN // rows,),
            in_specs=[
                pl.BlockSpec((slots, rows, enc), lambda i, s: (0, i, 0)),
                pl.BlockSpec((2 * PAD, width), lambda i, s: (0, 0)),
            ],
            out_specs=(
                pl.BlockSpec((database.shape[0], rows, enc), lambda i, s: (0, i, 0)),
                pl.BlockSpec((per_dev, width), lambda i, s: (0, 0)),
                pl.BlockSpec((per_dev, width), lambda i, s: (0, 0)),
            ),
        ),
        compiler_params=pltpu.CompilerParams(vmem_limit_bytes=VMEM_LIMIT),
    )(arrived, returned, wgrad)
    return context, query_grad, database_grad, key_part, value_part


def solution(mesh):
    return jax.shard_map(
        functools.partial(local, mesh.shape["dp"], mesh.shape["seq"]),
        mesh=mesh,
        in_specs=(
            P("dp", "seq", None),
            P("dp", "seq", None),
            P(("dp", "seq"), None, None),
            P(),
            P(),
            P("dp", "seq", None, None),
            P("dp", "seq", None, None),
        ),
        out_specs=(
            P("dp", "seq", None),
            P("dp", "seq", None),
            P(("dp", "seq"), None, None),
            P(("dp", "seq"), None),
            P(("dp", "seq"), None),
        ),
        check_vma=False,
    )
```

```python
import functools

import jax
import jax.numpy as jnp
from jax import lax
from jax.experimental import pallas as pl
from jax.experimental.pallas import tpu as pltpu
from jax.sharding import PartitionSpec as P

HD = 128
SPAN = 64
LAG = SPAN - 1
NB_LEN = 128
CAP = 2
PAD = 8
BF = jnp.bfloat16
F32 = jnp.float32
MESH = pl.DeviceIdType.MESH
VMEM_LIMIT = 62 * 2**20


def dims(n_dp, n_seq):
    side = int(round(n_seq**0.5))
    return n_dp // 2, side


def position():
    dp, seq = lax.axis_index("dp"), lax.axis_index("seq")
    return dp, seq, dp // 2, dp % 2


def toward(nz, rel):
    dp, seq, z, c = position()
    dz, dc = rel // 2, rel % 2
    return (lax.rem(z + dz, nz) * 2 + lax.rem(c + dc, 2), seq)


def back(nz, rel):
    dp, seq, z, c = position()
    dz, dc = rel // 2, rel % 2
    return (lax.rem(z + nz - dz, nz) * 2 + lax.rem(c + dc, 2), seq)


def along(side, first, step):
    dp, seq, z, c = position()
    y, x = seq // side, seq % side
    by_y = (1 - c) if first else c
    ny = lax.rem(y + step * by_y, side)
    nx = lax.rem(x + step * (1 - by_y), side)
    return (dp, ny * side + nx)


def greet(devices):
    barrier = pltpu.get_barrier_semaphore()
    for device in devices:
        pl.semaphore_signal(barrier, inc=1, device_id=device, device_id_type=MESH)
    pl.semaphore_wait(barrier, len(devices))


def remote(src, dst, send, recv, device):
    return pltpu.make_async_remote_copy(
        src_ref=src,
        dst_ref=dst,
        send_sem=send,
        recv_sem=recv,
        device_id=device,
        device_id_type=MESH,
    )


def far_first(nz):
    return sorted(range(2 * nz), key=lambda r: (-min(r // 2, nz - r // 2), r))


def nt(a, b):
    return lax.dot_general(a, b, (((1,), (1,)), ((), ())), preferred_element_type=F32)


def tn(a, b):
    return lax.dot_general(a, b, (((0,), (0,)), ((), ())), preferred_element_type=F32)


def nn(a, b):
    return jnp.dot(a, b, preferred_element_type=F32)


def main_kernel(
    nz, side,
    named, db_hbm, q_hbm, g_hbm, kw_hbm, vw_hbm,
    ctx_out, dq_out, tails_out, returned, arrived, wgrad,
    db, outb, inb, req, arr, arr_s, heads, q, g, qs, gs, kw, vw, kv, pg, ng, sa_k, sa_v, sb_k, sb_v, tails,
    r2, s3, r3,
    ld, rq_s, rq_r, ga_s, ga_r, hd_s, hd_r, own_sem, rt_s, rt_r, tl_s, tl_r,
    p0_s, p0_r, p1_s, p1_r, p2_s, p2_r, p3_s, p3_r, free0, free1,
):
    n_seq = side * side
    dp, seq, z, c = position()
    y, x = seq // side, seq % side
    before = (dp, lax.rem(seq + n_seq - 1, n_seq))
    after = (dp, lax.rem(seq + 1, n_seq))
    sibling = (z * 2 + (1 - c), seq)
    rels = [r for r in far_first(nz) if r]
    steps = range(1, side)
    loads = []
    pairs_in = ((db_hbm, db), (kw_hbm, kw), (vw_hbm, vw), (q_hbm, q), (g_hbm, g))
    for i, (src, dst) in enumerate(pairs_in):
        copy = pltpu.make_async_copy(src, dst, ld.at[i])
        copy.start()
        loads.append(copy)
    picks, blocks = named.shape[2], named.shape[3]
    refs = blocks * picks
    slots = CAP * 2 * nz
    held = db_hbm.shape[0]
    both = [named[0, 0, i % picks, i // picks] for i in range(refs)]
    target, row_of = [a // held for a in both], [a % held for a in both]
    slot = []
    for i in range(refs):
        rank = sum([jnp.where(target[j] == target[i], 1, 0) for j in range(i)], jnp.int32(0))
        dz = lax.rem(z + nz - target[i] // 2, nz)
        dc = lax.rem(c + target[i], 2)
        slot.append((dz * 2 + dc) * CAP + jnp.minimum(rank, CAP - 1))
    lane = lax.broadcasted_iota(jnp.int32, (8, 128), 1)
    source = []
    for r in range(2 * nz):
        tile = jnp.zeros((8, 128), jnp.int32)
        for k in range(CAP):
            here = [slot[i] == CAP * r + k for i in range(refs)]
            asked = sum([jnp.where(here[i], row_of[i] + 1, 0) for i in range(refs)], jnp.int32(0))
            mine = sum([jnp.where(here[i], i, 0) for i in range(refs)], jnp.int32(0))
            source.append(jnp.minimum(mine, refs - 1))
            tile = jnp.where(lane == k, asked - 1, tile)
        req[r] = tile
    greet(
        [toward(nz, r) for r in rels]
        + [along(side, True, s) for s in steps]
        + [along(side, False, s) for s in steps]
        + [before, after]
    )
    asks = []
    for r in rels:
        copy = remote(req.at[r], arr.at[r], rq_s.at[r], rq_r.at[r], back(nz, r))
        copy.start()
        asks.append(copy)
    arr[0] = req[0]
    head_copies = []
    for t, ref in enumerate((q_hbm, g_hbm)):
        copy = remote(ref.at[:, 0:SPAN], heads.at[t], hd_s.at[t], hd_r.at[t], before)
        copy.start()
        head_copies.append(copy)
    for copy in asks:
        copy.wait_recv()
    to_smem = pltpu.make_async_copy(arr, arr_s, ld.at[5])
    to_smem.start()
    loads[0].wait()
    to_smem.wait()
    last_row = db.shape[0] - 1
    sends = {}
    for r in rels:
        for k in range(CAP):
            row = jnp.clip(arr_s[r, 0, k], 0, last_row)
            outb[CAP * r + k] = db[row]
        part = pl.ds(CAP * r, CAP)
        copy = remote(outb.at[part], inb.at[part], ga_s.at[r], ga_r.at[r], toward(nz, r))
        copy.start()
        sends[r] = copy
    for k in range(CAP):
        row = jnp.clip(arr_s[0, 0, k], 0, last_row)
        inb[k] = db[row]
    for r in range(2 * nz):
        for k in range(CAP):
            arrived[CAP * r + k] = arr_s[r, 0, k]
    arrived[slots] = seq
    enc = db.shape[2]
    half_rows = PAD * nz * n_seq
    rows_2 = PAD * nz
    rows_1 = rows_2 * side
    piece = NB_LEN
    per_dev = enc // (2 * nz * n_seq)
    pieces = 2 * half_rows // piece
    for a in range(pieces):
        m = lax.broadcasted_iota(jnp.int32, (piece, 128), 0) + a * piece
        core, rest = m // half_rows, m % half_rows
        a1, a2, mz, row = rest // rows_1, (rest // rows_2) % side, (rest // PAD) % nz, rest % PAD
        cell = jnp.where(core == 0, a1 * side + a2, a2 * side + a1)
        column = ((mz * 2 + core) * n_seq + cell) * per_dev + row
        column = jnp.where(row < per_dev, column, enc)
        for o in range(0, enc, 128):
            hit = lax.broadcasted_iota(jnp.int32, (piece, 128), 1) + o == column
            db[a, :, o : o + 128] = jnp.where(hit, 1.0, 0.0).astype(BF)
    at_end = seq == n_seq - 1
    width = 256
    seqs, rows = q.shape[0], q.shape[1]
    per_seq = rows // SPAN
    for t, (ref, out) in enumerate(((q, qs), (g, gs))):
        loads[3 + t].wait()
        head_copies[t].wait_recv()
        for j in range(seqs):

            def shift(i, carry, ref=ref, out=out, t=t, j=j):
                lanes = pl.ds(pl.multiple_of(i * width, width), width)
                own = ref[j, :, lanes].astype(F32)
                head = heads[t, j, :, lanes].astype(F32)
                head = jnp.where(at_end, jnp.zeros_like(head), head)
                both = jnp.concatenate([own, head], axis=0)
                moved = pltpu.roll(both, rows + SPAN - LAG, 0)[:rows].astype(BF)
                for u in range(per_seq):
                    out[j * per_seq + u, :, lanes] = moved[u * SPAN : (u + 1) * SPAN]
                return carry

            lax.fori_loop(0, ref.shape[2] // width, shift, 0)
    hw = kw.shape[1]
    loads[1].wait()
    loads[2].wait()
    step_lanes = 512
    for r in [0, 1] + [r for r in rels if r != 1]:
        if r:
            sends[r].wait_recv()

        def project(i, carry, r=r):
            lanes = pl.ds(pl.multiple_of(i * step_lanes, step_lanes), step_lanes)
            later = pl.ds(pl.multiple_of(hw + i * step_lanes, step_lanes), step_lanes)
            rows_in = inb[CAP * r : CAP * (r + 1)].reshape(CAP * NB_LEN, enc)
            keys = nn(rows_in, kw[:, lanes]).astype(BF)
            kv[CAP * r : CAP * (r + 1), :, lanes] = keys.reshape(CAP, NB_LEN, step_lanes)
            values = nn(rows_in, vw[:, lanes]).astype(BF)
            kv[CAP * r : CAP * (r + 1), :, later] = values.reshape(CAP, NB_LEN, step_lanes)
            return carry

        lax.fori_loop(0, hw // step_lanes, project, 0)
    scale = HD**-0.5
    wide = 2 * HD
    first_head = lax.broadcasted_iota(jnp.int32, (SPAN, wide), 1) < HD

    def diagonal(a):
        zero = jnp.zeros_like(a)
        return jnp.concatenate(
            [jnp.where(first_head, a, zero), jnp.where(first_head, zero, a)], axis=0
        )

    def folded(a):
        return jnp.where(first_head, a[:SPAN], a[SPAN:]).astype(BF)

    def attend(hp, stage_k, stage_v, beside):
        lanes = pl.ds(pl.multiple_of(hp * wide, wide), wide)
        later = pl.ds(pl.multiple_of(hw + hp * wide, wide), wide)
        every = range(blocks)
        kb, vb, qd, gd = [], [], [], []
        for b in every:
            mine = [slot[picks * b + i] for i in range(picks)]
            kb.append(jnp.concatenate([kv[i, :, lanes] for i in mine], axis=0))
            vb.append(jnp.concatenate([kv[i, :, later] for i in mine], axis=0))
            qd.append(diagonal(qs[b, :, lanes]))
            gd.append(diagonal(gs[b, :, lanes]))
        scores = [nt(qd[b], kb[b]) for b in every]
        pgr = [nt(gd[b], vb[b]) for b in every]
        beside(0)
        p = []
        for b in every:
            e = jnp.exp(scores[b] * scale)
            p.append(e / jnp.sum(e, axis=1, keepdims=True))
        half = [p[b].astype(BF) for b in every]
        beside(1)
        out = [folded(nn(half[b], vb[b])) for b in every]
        value_g = [tn(half[b], gd[b]).astype(BF) for b in every]
        beside(2)
        ds = []
        for b in every:
            delta = jnp.sum(p[b] * pgr[b], axis=1, keepdims=True)
            ds.append((scale * p[b] * (pgr[b] - delta)).astype(BF))
        beside(3)
        back_out = [folded(nn(ds[b], kb[b])) for b in every]
        key_g = [tn(ds[b], qd[b]).astype(BF) for b in every]
        for b in every:
            rows_b = slice(b * picks * NB_LEN, (b + 1) * picks * NB_LEN)
            qs[b, :, lanes] = out[b]
            gs[b, :, lanes] = back_out[b]
            stage_k[rows_b] = key_g[b]
            stage_v[rows_b] = value_g[b]
            pg[picks * b : picks * (b + 1), :, lanes] = key_g[b].reshape(picks, NB_LEN, wide)
            pg[picks * b : picks * (b + 1), :, later] = value_g[b].reshape(picks, NB_LEN, wide)

    def add_near(hp, stage_k, stage_v):
        lanes = pl.ds(pl.multiple_of(hp * wide, wide), wide)

        def add(b):
            rows_b = slice(b * picks * NB_LEN, (b + 1) * picks * NB_LEN)
            ng[rows_b] += nt(stage_k[rows_b], kw[:, lanes]) + nt(stage_v[rows_b], vw[:, lanes])

        return add

    ng[...] = jnp.zeros_like(ng)
    sb_k[...] = jnp.zeros_like(sb_k)
    sb_v[...] = jnp.zeros_like(sb_v)

    def tail_copy(i, t, j):
        lanes = pl.ds(pl.multiple_of(i * 2 * wide, 2 * wide), 2 * wide)
        return remote(
            (qs, gs)[t].at[per_seq * (j + 1) - 1, :, lanes], tails.at[t, j, :, lanes],
            tl_s.at[i, t, j], tl_r.at[i, t, j], after,
        )

    def two_pairs(i, carry):
        attend(2 * i, sa_k, sa_v, add_near(jnp.maximum(2 * i - 1, 0), sb_k, sb_v))
        attend(2 * i + 1, sb_k, sb_v, add_near(2 * i, sa_k, sa_v))
        for t in range(2):
            for j in range(seqs):
                tail_copy(i, t, j).start()
        return carry

    lax.fori_loop(0, hw // (2 * wide), two_pairs, 0)
    last = add_near(hw // wide - 1, sb_k, sb_v)
    for b in range(blocks):
        last(b)
    for i in range(refs):
        db[pieces + i] = ng[i * NB_LEN : (i + 1) * NB_LEN].astype(BF)
    pl.semaphore_signal(free0, inc=1, device_id=sibling, device_id_type=MESH)
    for s in steps:
        pl.semaphore_signal(free1, inc=1, device_id=along(side, True, s), device_id_type=MESH)
    for copy in sends.values():
        copy.wait_send()
    return_copies = []

    def give_back(r):
        for k in range(CAP):
            outb[CAP * r + k] = db[pieces + source[CAP * r + k]]
        part = pl.ds(CAP * r, CAP)
        if r:
            copy = remote(outb.at[part], returned.at[part], rt_s.at[r], rt_r.at[r], back(nz, r))
            return_copies.append(copy)
        else:
            copy = pltpu.make_async_copy(outb.at[part], returned.at[part], own_sem)
            own_copies.append(copy)
        copy.start()

    own_copies = []
    chunks = p0_s.shape[0]
    cw = 2 * hw // chunks
    my1 = jnp.where(c == 0, y, x)
    my2 = jnp.where(c == 0, x, y)
    phase0, phase1, phase2, phase3 = [], [], [], []

    def rows_of(a):
        return pl.ds(pl.multiple_of(a * rows_2, rows_2), rows_2)

    def lanes_of(a):
        return pl.ds(pl.multiple_of(a * cw, cw), cw)

    def product(core, i, base):
        start = pl.multiple_of(core * half_rows, half_rows)
        some = jnp.concatenate([part[pl.ds(start, half_rows)] for part in near_t], axis=1)
        for o in range(0, cw, step_lanes):
            these = pg[:, :, i * cw + o : i * cw + o + step_lanes]
            out = nn(some, these.reshape(refs * NB_LEN, step_lanes)).astype(BF)
            for a in range(side):
                kv[base + i, :, a * cw + o : a * cw + o + step_lanes] = out[
                    a * rows_1 : (a + 1) * rows_1
                ]

    def multiply(i):
        product(1 - c, i, 0)
        if i == 0:
            pl.semaphore_wait(free0, 1)
        copy = remote(kv.at[i], kv.at[2 * chunks + i], p0_s.at[i], p0_r.at[i], sibling)
        copy.start()
        phase0.append(copy)
        product(c, i, chunks)

    def send_first(i):
        phase0[i].wait_recv()
        kv[chunks + i] = (kv[chunks + i].astype(F32) + kv[2 * chunks + i].astype(F32)).astype(BF)
        if i == 0:
            pl.semaphore_wait(free1, side - 1)
        out = []
        for s in steps:
            to = lax.rem(my1 + s, side)
            copy = remote(
                kv.at[chunks + i, :, lanes_of(to)],
                kv.at[3 * chunks + i, :, pl.ds((s - 1) * cw, cw)],
                p1_s.at[i, s - 1], p1_r.at[i, s - 1], along(side, True, s),
            )
            copy.start()
            out.append(copy)
        phase1.append(out)

    for r in rels + [0]:
        give_back(r)
    outs = []
    for t, (ref, hbm) in enumerate(((qs, ctx_out), (gs, dq_out))):
        copy = pltpu.make_async_copy(ref, hbm, ld.at[6 + t])
        copy.start()
        outs.append(copy)
    near_t = (sa_k, sa_v, sb_k, sb_v)
    for i in range(0, refs, 2):
        both = jnp.concatenate([inb[slot[i]], inb[slot[i + 1]]], axis=0)
        near_t[i // 2][...] = nt(db[0:pieces].reshape(2 * half_rows, enc), both).astype(BF)
    for i in range(chunks + 1):
        if i < chunks:
            multiply(i)
        if i:
            send_first(i - 1)
    tail_copies = [
        tail_copy(i, t, j)
        for t in range(2)
        for j in range(seqs)
        for i in range(hw // (2 * wide))
    ]
    for copy in tail_copies:
        copy.wait_recv()
    copy = pltpu.make_async_copy(tails, tails_out, ld.at[8])
    copy.start()
    outs.append(copy)
    for i in range(chunks):
        total = kv[chunks + i, :, lanes_of(my1)].astype(F32)
        for s in steps:
            phase1[i][s - 1].wait_recv()
            total = total + kv[3 * chunks + i, :, (s - 1) * cw : s * cw].astype(F32)
        kv[3 * chunks + i, :, (side - 1) * cw : side * cw] = total.astype(BF)
        out = []
        for s in steps:
            to = lax.rem(my2 + s, side)
            copy = remote(
                kv.at[3 * chunks + i, rows_of(to), pl.ds((side - 1) * cw, cw)], r2.at[i, s - 1], p2_s.at[i, s - 1], p2_r.at[i, s - 1],
                along(side, False, s),
            )
            copy.start()
            out.append(copy)
        phase2.append(out)
    totals = []
    for i in range(chunks):
        total = kv[3 * chunks + i, rows_of(my2), (side - 1) * cw : side * cw].astype(F32)
        for s in steps:
            phase2[i][s - 1].wait_recv()
            total = total + r2[i, s - 1].astype(F32)
        totals.append(total)
        if i >= chunks // 2:
            a = i - chunks // 2
            for part in range(nz):
                row = slice(part * PAD, (part + 1) * PAD)
                both = jnp.concatenate([totals[a][row], total[row]], axis=0)
                s3[part, :, a * cw : (a + 1) * cw] = both.astype(BF)
    for s in range(1, nz):
        copy = remote(
            s3.at[lax.rem(z + s, nz)], r3.at[s - 1], p3_s.at[s - 1], p3_r.at[s - 1],
            (lax.rem(z + s, nz) * 2 + c, seq),
        )
        copy.start()
        phase3.append(copy)
    total = s3[z].astype(F32)
    for s in range(1, nz):
        phase3[s - 1].wait_recv()
        total = total + r3[s - 1].astype(F32)
    wgrad[...] = total
    for copy in outs + own_copies:
        copy.wait()
    for copy in return_copies:
        copy.wait_recv()
    for copy in (
        asks + head_copies + return_copies + tail_copies + phase0
        + sum(phase1, []) + sum(phase2, []) + phase3
    ):
        copy.wait_send()


def finish_kernel(
    arrived, returned, wgrad, ctx, dq, tails, out, key_part, value_part, context, query_grad
):
    @pl.when(pl.program_id(0) == 0)
    def _():
        per_dev = key_part.shape[0]
        key_part[...] = wgrad[0:per_dev]
        value_part[...] = wgrad[PAD : PAD + per_dev]

    slots, seqs = returned.shape[0], tails.shape[1]
    per_seq = ctx.shape[0] // seqs
    rows = per_seq * SPAN
    at_start = arrived[slots] == 0
    for t, (ref, here) in enumerate(((ctx, context), (dq, query_grad))):
        for j in range(seqs):
            tail = tails[t, j].astype(F32)
            tail = jnp.where(at_start, jnp.zeros_like(tail), tail)
            own = [ref[per_seq * j + u].astype(F32) for u in range(per_seq)]
            both = jnp.concatenate([tail] + own, axis=0)
            here[j] = pltpu.roll(both, rows + LAG, 0)[:rows].astype(BF)
    out[...] = jnp.zeros_like(out)
    for s in range(slots):
        row = arrived[s]
        part = returned[s].astype(F32)
        out[jnp.clip(row, 0, out.shape[0] - 1)] += jnp.where(row >= 0, part, jnp.zeros_like(part))


def local(n_dp, n_seq, queries, d_context, database, key_weight, value_weight, shard, wanted):
    nz, side = dims(n_dp, n_seq)
    seqs, span, width = queries.shape
    blocks = seqs * span // SPAN
    refs = blocks * shard.shape[-1]
    slots = n_dp * CAP
    enc = database.shape[2]
    vmem = pl.BlockSpec(memory_space=pltpu.VMEM)
    smem = pl.BlockSpec(memory_space=pltpu.SMEM)
    anywhere = pl.BlockSpec(memory_space=pl.ANY)
    dma = pltpu.SemaphoreType.DMA
    regular = pltpu.SemaphoreType.REGULAR
    rows_2 = PAD * nz
    chunks = 4
    chunk = 2 * width // chunks
    more = side - 1
    ctx, dq, tails, returned, arrived, wgrad = pl.pallas_call(
        functools.partial(main_kernel, nz, side),
        name="main",
        out_shape=(
            jax.ShapeDtypeStruct((blocks, SPAN, width), BF),
            jax.ShapeDtypeStruct((blocks, SPAN, width), BF),
            jax.ShapeDtypeStruct((2, seqs, SPAN, width), BF),
            jax.ShapeDtypeStruct((slots, NB_LEN, enc), BF),
            jax.ShapeDtypeStruct((slots + 1,), jnp.int32),
            jax.ShapeDtypeStruct((2 * PAD, width), F32),
        ),
        in_specs=[smem] + [anywhere] * 5,
        out_specs=(anywhere, anywhere, anywhere, anywhere, smem, vmem),
        scratch_shapes=[
            pltpu.VMEM((database.shape[0], NB_LEN, enc), BF),
            pltpu.VMEM((slots, NB_LEN, enc), BF),
            pltpu.VMEM((slots, NB_LEN, enc), BF),
            pltpu.VMEM((n_dp, 8, 128), jnp.int32),
            pltpu.VMEM((n_dp, 8, 128), jnp.int32),
            pltpu.SMEM((n_dp, 8, 128), jnp.int32),
            pltpu.VMEM((2, seqs, SPAN, width), BF),
            pltpu.VMEM((seqs, span, width), BF),
            pltpu.VMEM((seqs, span, width), BF),
            pltpu.VMEM((blocks, SPAN, width), BF),
            pltpu.VMEM((blocks, SPAN, width), BF),
            pltpu.VMEM((enc, width), BF),
            pltpu.VMEM((enc, width), BF),
            pltpu.VMEM((slots, NB_LEN, 2 * width), BF),
            pltpu.VMEM((refs, NB_LEN, 2 * width), BF),
            pltpu.VMEM((refs * NB_LEN, enc), F32),
            pltpu.VMEM((refs * NB_LEN, 2 * HD), BF),
            pltpu.VMEM((refs * NB_LEN, 2 * HD), BF),
            pltpu.VMEM((refs * NB_LEN, 2 * HD), BF),
            pltpu.VMEM((refs * NB_LEN, 2 * HD), BF),
            pltpu.VMEM((2, seqs, SPAN, width), BF),
            pltpu.VMEM((chunks, more, rows_2, chunk), BF),
            pltpu.VMEM((nz, 2 * PAD, width), BF),
            pltpu.VMEM((nz - 1, 2 * PAD, width), BF),
            dma((9,)),
            dma((n_dp,)),
            dma((n_dp,)),
            dma((n_dp,)),
            dma((n_dp,)),
            dma((2,)),
            dma((2,)),
            dma,
            dma((n_dp,)),
            dma((n_dp,)),
            dma((width // (4 * HD), 2, seqs)),
            dma((width // (4 * HD), 2, seqs)),
            dma((chunks,)),
            dma((chunks,)),
            dma((chunks, more)),
            dma((chunks, more)),
            dma((chunks, more)),
            dma((chunks, more)),
            dma((nz - 1,)),
            dma((nz - 1,)),
            regular,
            regular,
        ],
        compiler_params=pltpu.CompilerParams(
            collective_id=0, has_side_effects=True, vmem_limit_bytes=VMEM_LIMIT
        ),
    )((shard * database.shape[0] + wanted).swapaxes(2, 3), database, queries, d_context, key_weight, value_weight)
    rows = 32
    per_dev = enc // (n_dp * n_seq)
    part = jax.ShapeDtypeStruct((per_dev, width), F32)
    steps = NB_LEN // rows
    lanes = width // steps
    placed = jax.ShapeDtypeStruct(queries.shape, BF)
    database_grad, key_part, value_part, context, query_grad = pl.pallas_call(
        finish_kernel,
        name="finish",
        out_shape=(jax.ShapeDtypeStruct(database.shape, F32), part, part, placed, placed),
        grid_spec=pltpu.PrefetchScalarGridSpec(
            num_scalar_prefetch=1,
            grid=(steps,),
            in_specs=[
                pl.BlockSpec((slots, rows, enc), lambda i, s: (0, i, 0)),
                pl.BlockSpec((2 * PAD, width), lambda i, s: (0, 0)),
                pl.BlockSpec((blocks, SPAN, lanes), lambda i, s: (0, 0, i)),
                pl.BlockSpec((blocks, SPAN, lanes), lambda i, s: (0, 0, i)),
                pl.BlockSpec((2, seqs, SPAN, lanes), lambda i, s: (0, 0, 0, i)),
            ],
            out_specs=(
                pl.BlockSpec((database.shape[0], rows, enc), lambda i, s: (0, i, 0)),
                pl.BlockSpec((per_dev, width), lambda i, s: (0, 0)),
                pl.BlockSpec((per_dev, width), lambda i, s: (0, 0)),
                pl.BlockSpec((seqs, span, lanes), lambda i, s: (0, 0, i)),
                pl.BlockSpec((seqs, span, lanes), lambda i, s: (0, 0, i)),
            ),
        ),
        compiler_params=pltpu.CompilerParams(vmem_limit_bytes=VMEM_LIMIT),
    )(arrived, returned, wgrad, ctx, dq, tails)
    return context, query_grad, database_grad, key_part, value_part


def solution(mesh):
    return jax.shard_map(
        functools.partial(local, mesh.shape["dp"], mesh.shape["seq"]),
        mesh=mesh,
        in_specs=(
            P("dp", "seq", None),
            P("dp", "seq", None),
            P(("dp", "seq"), None, None),
            P(),
            P(),
            P("dp", "seq", None, None),
            P("dp", "seq", None, None),
        ),
        out_specs=(
            P("dp", "seq", None),
            P("dp", "seq", None),
            P(("dp", "seq"), None, None),
            P(("dp", "seq"), None),
            P(("dp", "seq"), None),
        ),
        check_vma=False,
    )
```

```python
import functools

import jax
import jax.numpy as jnp
from jax import lax
from jax.experimental import pallas as pl
from jax.experimental.pallas import tpu as pltpu
from jax.sharding import PartitionSpec as P

HD = 128
SPAN = 64
LAG = SPAN - 1
NB_LEN = 128
CAP = 2
PAD = 8
BF = jnp.bfloat16
F32 = jnp.float32
MESH = pl.DeviceIdType.MESH
VMEM_LIMIT = 62 * 2**20


def dims(n_dp, n_seq):
    side = int(round(n_seq**0.5))
    return n_dp // 2, side


def position():
    dp, seq = lax.axis_index("dp"), lax.axis_index("seq")
    return dp, seq, dp // 2, dp % 2


def toward(nz, rel):
    dp, seq, z, c = position()
    dz, dc = rel // 2, rel % 2
    return (lax.rem(z + dz, nz) * 2 + lax.rem(c + dc, 2), seq)


def back(nz, rel):
    dp, seq, z, c = position()
    dz, dc = rel // 2, rel % 2
    return (lax.rem(z + nz - dz, nz) * 2 + lax.rem(c + dc, 2), seq)


def along(side, first, step):
    dp, seq, z, c = position()
    y, x = seq // side, seq % side
    by_y = (1 - c) if first else c
    ny = lax.rem(y + step * by_y, side)
    nx = lax.rem(x + step * (1 - by_y), side)
    return (dp, ny * side + nx)


def greet(devices):
    barrier = pltpu.get_barrier_semaphore()
    for device in devices:
        pl.semaphore_signal(barrier, inc=1, device_id=device, device_id_type=MESH)
    pl.semaphore_wait(barrier, len(devices))


def remote(src, dst, send, recv, device):
    return pltpu.make_async_remote_copy(
        src_ref=src,
        dst_ref=dst,
        send_sem=send,
        recv_sem=recv,
        device_id=device,
        device_id_type=MESH,
    )


def far_first(nz):
    return sorted(range(2 * nz), key=lambda r: (-min(r // 2, nz - r // 2), r))


def nt(a, b):
    return lax.dot_general(a, b, (((1,), (1,)), ((), ())), preferred_element_type=F32)


def tn(a, b):
    return lax.dot_general(a, b, (((0,), (0,)), ((), ())), preferred_element_type=F32)


def nn(a, b):
    return jnp.dot(a, b, preferred_element_type=F32)


def main_kernel(
    nz, side,
    shard, wanted, db_hbm, q_hbm, g_hbm, kw_hbm, vw_hbm,
    ctx_out, dq_out, tails_out, returned, arrived, wgrad,
    db, outb, inb, req, arr, arr_s, heads, q, g, qs, gs, kw, vw, kv, pg, ng, sa_k, sa_v, sb_k, sb_v, tails,
    r2, s3, r3,
    ld, rq_s, rq_r, ga_s, ga_r, hd_s, hd_r, own_sem, rt_s, rt_r, tl_s, tl_r,
    p0_s, p0_r, p1_s, p1_r, p2_s, p2_r, p3_s, p3_r, free0, free1,
):
    n_seq = side * side
    dp, seq, z, c = position()
    y, x = seq // side, seq % side
    before = (dp, lax.rem(seq + n_seq - 1, n_seq))
    after = (dp, lax.rem(seq + 1, n_seq))
    sibling = (z * 2 + (1 - c), seq)
    rels = [r for r in far_first(nz) if r]
    steps = range(1, side)
    loads = []
    pairs_in = ((db_hbm, db), (kw_hbm, kw), (vw_hbm, vw), (q_hbm, q), (g_hbm, g))
    for i, (src, dst) in enumerate(pairs_in):
        copy = pltpu.make_async_copy(src, dst, ld.at[i])
        copy.start()
        loads.append(copy)
    picks, blocks = shard.shape[2], shard.shape[3]
    refs = blocks * picks
    near_by = 2 * nz
    slots = CAP * near_by
    named = [[shard[0, 0, i, b] for i in range(picks)] for b in range(blocks)]
    order = [jnp.int32(b) for b in range(blocks)]
    for e0 in reversed(range(blocks)):
        for e1 in reversed(range(e0 + 1, blocks)):
            apart = 0
            for i in named[e0]:
                for j in named[e1]:
                    apart = apart + jnp.where(i == j, 1, 0)
            wish = [e0, e1] + [b for b in range(blocks) if b not in (e0, e1)]
            order = [jnp.where(apart == 0, w, o) for w, o in zip(wish, order)]
    place = [
        sum([jnp.where(order[n] == b, n, 0) for n in range(blocks)], jnp.int32(0))
        for b in range(blocks)
    ]
    target = [shard[0, 0, i % picks, order[i // picks]] for i in range(refs)]
    row_of = [wanted[0, 0, i % picks, order[i // picks]] for i in range(refs)]
    slot = []
    for i in range(refs):
        rank = sum([jnp.where(target[j] == target[i], 1, 0) for j in range(i)], jnp.int32(0))
        dz = lax.rem(z + nz - target[i] // 2, nz)
        dc = lax.rem(c + target[i], 2)
        slot.append(jnp.minimum(rank, CAP - 1) * near_by + dz * 2 + dc)
    lane = lax.broadcasted_iota(jnp.int32, (8, 128), 1)
    source = {}
    for r in range(2 * nz):
        tile = jnp.zeros((8, 128), jnp.int32)
        for k in range(CAP):
            here = [slot[i] == k * near_by + r for i in range(refs)]
            asked = sum([jnp.where(here[i], row_of[i] + 1, 0) for i in range(refs)], jnp.int32(0))
            mine = sum([jnp.where(here[i], i, 0) for i in range(refs)], jnp.int32(0))
            source[k, r] = jnp.minimum(mine, refs - 1)
            tile = jnp.where(lane == k, asked - 1, tile)
        req[r] = tile
    greet(
        [toward(nz, r) for r in rels]
        + [along(side, True, s) for s in steps]
        + [along(side, False, s) for s in steps]
        + [before, after]
    )
    asks = []
    for r in rels:
        copy = remote(req.at[r], arr.at[r], rq_s.at[r], rq_r.at[r], back(nz, r))
        copy.start()
        asks.append(copy)
    arr[0] = req[0]
    head_copies = []
    for t, ref in enumerate((q_hbm, g_hbm)):
        copy = remote(ref.at[:, 0:SPAN], heads.at[t], hd_s.at[t], hd_r.at[t], before)
        copy.start()
        head_copies.append(copy)
    for copy in asks:
        copy.wait_recv()
    to_smem = pltpu.make_async_copy(arr, arr_s, ld.at[5])
    to_smem.start()
    loads[0].wait()
    to_smem.wait()
    last_row = db.shape[0] - 1
    sends = {}
    first_sent = [1] + [r for r in rels if r != 1]
    for k in range(CAP):
        for r in first_sent:
            here = k * near_by + r
            row = jnp.clip(arr_s[r, 0, k], 0, last_row)
            outb[here] = db[row]
            copy = remote(
                outb.at[here], inb.at[here], ga_s.at[k, r], ga_r.at[k, r], toward(nz, r)
            )
            copy.start()
            sends[k, r] = copy
    for k in range(CAP):
        row = jnp.clip(arr_s[0, 0, k], 0, last_row)
        inb[k * near_by] = db[row]
    for r in range(near_by):
        for k in range(CAP):
            arrived[k * near_by + r] = arr_s[r, 0, k]
    arrived[slots] = seq
    for b in range(blocks):
        arrived[slots + 1 + b] = place[b]
    enc = db.shape[2]
    half_rows = PAD * nz * n_seq
    rows_2 = PAD * nz
    rows_1 = rows_2 * side
    piece = NB_LEN
    per_dev = enc // (2 * nz * n_seq)
    pieces = 2 * half_rows // piece
    for a in range(pieces):
        m = lax.broadcasted_iota(jnp.int32, (piece, 128), 0) + a * piece
        core, rest = m // half_rows, m % half_rows
        a1, a2, mz, row = rest // rows_1, (rest // rows_2) % side, (rest // PAD) % nz, rest % PAD
        cell = jnp.where(core == 0, a1 * side + a2, a2 * side + a1)
        column = ((mz * 2 + core) * n_seq + cell) * per_dev + row
        column = jnp.where(row < per_dev, column, enc)
        for o in range(0, enc, 128):
            hit = lax.broadcasted_iota(jnp.int32, (piece, 128), 1) + o == column
            db[a, :, o : o + 128] = jnp.where(hit, 1.0, 0.0).astype(BF)
    at_end = seq == n_seq - 1
    width = 256
    seqs, rows = q.shape[0], q.shape[1]
    per_seq = rows // SPAN
    for t in range(2):
        loads[3 + t].wait()
        head_copies[t].wait_recv()
    for t, (ref, out) in enumerate(((q, qs), (g, gs))):
        for n in range(blocks):

            def shift(i, carry, ref=ref, out=out, t=t, n=n):
                lanes = pl.ds(pl.multiple_of(i * width, width), width)
                j, u = order[n] // per_seq, order[n] % per_seq
                own = ref[j, :, lanes].astype(F32)
                head = heads[t, j, :, lanes].astype(F32)
                head = jnp.where(at_end, jnp.zeros_like(head), head)
                both = jnp.concatenate([own, head], axis=0)
                moved = pltpu.roll(both, rows + SPAN - LAG, 0)
                chosen = moved[:SPAN]
                for v in range(1, per_seq):
                    chosen = jnp.where(u == v, moved[v * SPAN : (v + 1) * SPAN], chosen)
                out[n, :, lanes] = chosen.astype(BF)
                return carry

            lax.fori_loop(0, ref.shape[2] // width, shift, 0)
    hw = kw.shape[1]
    loads[1].wait()
    loads[2].wait()
    step_lanes = 512

    def arrive(k):
        for m in [0] + sorted(range(1, nz), key=lambda m: (-min(m, nz - m), m)):
            for r in (2 * m, 2 * m + 1):
                if r:
                    sends[k, r].wait_recv()
            first = k * near_by + 2 * m
            pair_of = slice(first, first + 2)

            def project(i, carry, pair_of=pair_of):
                lanes = pl.ds(pl.multiple_of(i * step_lanes, step_lanes), step_lanes)
                later = pl.ds(pl.multiple_of(hw + i * step_lanes, step_lanes), step_lanes)
                rows_in = inb[pair_of].reshape(2 * NB_LEN, enc)
                keys = nn(rows_in, kw[:, lanes]).astype(BF)
                kv[pair_of, :, lanes] = keys.reshape(2, NB_LEN, step_lanes)
                values = nn(rows_in, vw[:, lanes]).astype(BF)
                kv[pair_of, :, later] = values.reshape(2, NB_LEN, step_lanes)
                return carry

            lax.fori_loop(0, hw // step_lanes, project, 0)

    scale = HD**-0.5
    wide = 2 * HD
    first_head = lax.broadcasted_iota(jnp.int32, (SPAN, wide), 1) < HD

    def diagonal(a):
        zero = jnp.zeros_like(a)
        return jnp.concatenate(
            [jnp.where(first_head, a, zero), jnp.where(first_head, zero, a)], axis=0
        )

    def folded(a):
        return jnp.where(first_head, a[:SPAN], a[SPAN:]).astype(BF)

    def attend(every, hp, stage_k, stage_v, beside):
        lanes = pl.ds(pl.multiple_of(hp * wide, wide), wide)
        later = pl.ds(pl.multiple_of(hw + hp * wide, wide), wide)
        kb, vb, qd, gd = {}, {}, {}, {}
        for b in every:
            mine = [slot[picks * b + i] for i in range(picks)]
            kb[b] = jnp.concatenate([kv[i, :, lanes] for i in mine], axis=0)
            vb[b] = jnp.concatenate([kv[i, :, later] for i in mine], axis=0)
            qd[b] = diagonal(qs[b, :, lanes])
            gd[b] = diagonal(gs[b, :, lanes])
        scores = {b: nt(qd[b], kb[b]) for b in every}
        pgr = {b: nt(gd[b], vb[b]) for b in every}
        beside(0)
        p = {}
        for b in every:
            e = jnp.exp(scores[b] * scale)
            p[b] = e / jnp.sum(e, axis=1, keepdims=True)
        half = {b: p[b].astype(BF) for b in every}
        beside(1)
        out = {b: folded(nn(half[b], vb[b])) for b in every}
        value_g = {b: tn(half[b], gd[b]).astype(BF) for b in every}
        beside(2)
        ds = {}
        for b in every:
            delta = jnp.sum(p[b] * pgr[b], axis=1, keepdims=True)
            ds[b] = (scale * p[b] * (pgr[b] - delta)).astype(BF)
        beside(3)
        back_out = {b: folded(nn(ds[b], kb[b])) for b in every}
        key_g = {b: tn(ds[b], qd[b]).astype(BF) for b in every}
        for b in every:
            rows_b = slice(b * picks * NB_LEN, (b + 1) * picks * NB_LEN)
            qs[b, :, lanes] = out[b]
            gs[b, :, lanes] = back_out[b]
            stage_k[rows_b] = key_g[b]
            stage_v[rows_b] = value_g[b]
            pg[picks * b : picks * (b + 1), :, lanes] = key_g[b].reshape(picks, NB_LEN, wide)
            pg[picks * b : picks * (b + 1), :, later] = value_g[b].reshape(picks, NB_LEN, wide)

    def add_near(every, hp, stage_k, stage_v):
        lanes = pl.ds(pl.multiple_of(hp * wide, wide), wide)

        def add(step):
            if step % 2 or step // 2 >= len(every):
                return
            b = every[step // 2]
            rows_b = slice(b * picks * NB_LEN, (b + 1) * picks * NB_LEN)
            ng[rows_b] += nt(stage_k[rows_b], kw[:, lanes]) + nt(stage_v[rows_b], vw[:, lanes])

        return add

    ng[...] = jnp.zeros_like(ng)
    sb_k[...] = jnp.zeros_like(sb_k)
    sb_v[...] = jnp.zeros_like(sb_v)

    def tail_copy(i, t, j):
        lanes = pl.ds(pl.multiple_of(i * 2 * wide, 2 * wide), 2 * wide)
        return remote(
            heads.at[t, j, :, lanes], tails.at[t, j, :, lanes],
            tl_s.at[i, t, j], tl_r.at[i, t, j], after,
        )

    def half_of(every, at_last):
        def two_pairs(i, carry):
            attend(
                every, 2 * i, sa_k, sa_v, add_near(every, jnp.maximum(2 * i - 1, 0), sb_k, sb_v)
            )
            attend(every, 2 * i + 1, sb_k, sb_v, add_near(every, 2 * i, sa_k, sa_v))
            if at_last:
                lanes = pl.ds(pl.multiple_of(i * 2 * wide, 2 * wide), 2 * wide)
                for t, ref in enumerate((qs, gs)):
                    for j in range(seqs):
                        heads[t, j, :, lanes] = ref[place[per_seq * (j + 1) - 1], :, lanes]
                        tail_copy(i, t, j).start()
            return carry

        lax.fori_loop(0, hw // (2 * wide), two_pairs, 0)
        last = add_near(every, hw // wide - 1, sb_k, sb_v)
        for step in range(2 * len(every)):
            last(step)

    for k in range(CAP):
        arrive(k)
        half_of([2 * k, 2 * k + 1], k == CAP - 1)
    for i in range(refs):
        db[pieces + i] = ng[i * NB_LEN : (i + 1) * NB_LEN].astype(BF)
    pl.semaphore_signal(free0, inc=1, device_id=sibling, device_id_type=MESH)
    for s in steps:
        pl.semaphore_signal(free1, inc=1, device_id=along(side, True, s), device_id_type=MESH)
    for copy in sends.values():
        copy.wait_send()
    return_copies = []

    def give_back(k, r):
        here = k * near_by + r
        outb[here] = db[pieces + source[k, r]]
        if r:
            copy = remote(
                outb.at[here], returned.at[here], rt_s.at[k, r], rt_r.at[k, r], back(nz, r)
            )
            return_copies.append(copy)
        else:
            copy = pltpu.make_async_copy(outb.at[here], returned.at[here], own_sem.at[k])
            own_copies.append(copy)
        copy.start()

    own_copies = []
    chunks = p0_s.shape[0]
    cw = 2 * hw // chunks
    my1 = jnp.where(c == 0, y, x)
    my2 = jnp.where(c == 0, x, y)
    phase0, phase1, phase2, phase3 = [], [], [], []

    def rows_of(a):
        return pl.ds(pl.multiple_of(a * rows_2, rows_2), rows_2)

    def lanes_of(a):
        return pl.ds(pl.multiple_of(a * cw, cw), cw)

    def product(core, i, base):
        start = pl.multiple_of(core * half_rows, half_rows)
        some = jnp.concatenate([part[pl.ds(start, half_rows)] for part in near_t], axis=1)
        for o in range(0, cw, step_lanes):
            these = pg[:, :, i * cw + o : i * cw + o + step_lanes]
            out = nn(some, these.reshape(refs * NB_LEN, step_lanes)).astype(BF)
            for a in range(side):
                kv[base + i, :, a * cw + o : a * cw + o + step_lanes] = out[
                    a * rows_1 : (a + 1) * rows_1
                ]

    def multiply(i):
        product(1 - c, i, 0)
        if i == 0:
            pl.semaphore_wait(free0, 1)
        copy = remote(kv.at[i], kv.at[2 * chunks + i], p0_s.at[i], p0_r.at[i], sibling)
        copy.start()
        phase0.append(copy)
        product(c, i, chunks)

    def send_first(i):
        phase0[i].wait_recv()
        kv[chunks + i] = (kv[chunks + i].astype(F32) + kv[2 * chunks + i].astype(F32)).astype(BF)
        if i == 0:
            pl.semaphore_wait(free1, side - 1)
        out = []
        for s in steps:
            to = lax.rem(my1 + s, side)
            copy = remote(
                kv.at[chunks + i, :, lanes_of(to)],
                kv.at[3 * chunks + i, :, pl.ds((s - 1) * cw, cw)],
                p1_s.at[i, s - 1], p1_r.at[i, s - 1], along(side, True, s),
            )
            copy.start()
            out.append(copy)
        phase1.append(out)

    for r in rels + [0]:
        for k in range(CAP):
            give_back(k, r)
    outs = []
    for t, (ref, hbm) in enumerate(((qs, ctx_out), (gs, dq_out))):
        copy = pltpu.make_async_copy(ref, hbm, ld.at[6 + t])
        copy.start()
        outs.append(copy)
    near_t = (sa_k, sa_v, sb_k, sb_v)
    for i in range(0, refs, 2):
        both = jnp.concatenate([inb[slot[i]], inb[slot[i + 1]]], axis=0)
        near_t[i // 2][...] = nt(db[0:pieces].reshape(2 * half_rows, enc), both).astype(BF)
    for i in range(chunks + 1):
        if i < chunks:
            multiply(i)
        if i:
            send_first(i - 1)
    tail_copies = [
        tail_copy(i, t, j)
        for t in range(2)
        for j in range(seqs)
        for i in range(hw // (2 * wide))
    ]
    for copy in tail_copies:
        copy.wait_recv()
    copy = pltpu.make_async_copy(tails, tails_out, ld.at[8])
    copy.start()
    outs.append(copy)
    for i in range(chunks):
        total = kv[chunks + i, :, lanes_of(my1)].astype(F32)
        for s in steps:
            phase1[i][s - 1].wait_recv()
            total = total + kv[3 * chunks + i, :, (s - 1) * cw : s * cw].astype(F32)
        kv[3 * chunks + i, :, (side - 1) * cw : side * cw] = total.astype(BF)
        out = []
        for s in steps:
            to = lax.rem(my2 + s, side)
            copy = remote(
                kv.at[3 * chunks + i, rows_of(to), pl.ds((side - 1) * cw, cw)], r2.at[i, s - 1], p2_s.at[i, s - 1], p2_r.at[i, s - 1],
                along(side, False, s),
            )
            copy.start()
            out.append(copy)
        phase2.append(out)
    totals = []
    for i in range(chunks):
        total = kv[3 * chunks + i, rows_of(my2), (side - 1) * cw : side * cw].astype(F32)
        for s in steps:
            phase2[i][s - 1].wait_recv()
            total = total + r2[i, s - 1].astype(F32)
        totals.append(total)
        if i >= chunks // 2:
            a = i - chunks // 2
            for part in range(nz):
                row = slice(part * PAD, (part + 1) * PAD)
                both = jnp.concatenate([totals[a][row], total[row]], axis=0)
                s3[part, :, a * cw : (a + 1) * cw] = both.astype(BF)
    for s in range(1, nz):
        copy = remote(
            s3.at[lax.rem(z + s, nz)], r3.at[s - 1], p3_s.at[s - 1], p3_r.at[s - 1],
            (lax.rem(z + s, nz) * 2 + c, seq),
        )
        copy.start()
        phase3.append(copy)
    total = s3[z].astype(F32)
    for s in range(1, nz):
        phase3[s - 1].wait_recv()
        total = total + r3[s - 1].astype(F32)
    wgrad[...] = total
    for copy in outs + own_copies:
        copy.wait()
    for copy in return_copies:
        copy.wait_recv()
    for copy in (
        asks + head_copies + return_copies + tail_copies + phase0
        + sum(phase1, []) + sum(phase2, []) + phase3
    ):
        copy.wait_send()


def finish_kernel(
    arrived, returned, wgrad, ctx, dq, tails, out, key_part, value_part, context, query_grad
):
    @pl.when(pl.program_id(0) == 0)
    def _():
        per_dev = key_part.shape[0]
        key_part[...] = wgrad[0:per_dev]
        value_part[...] = wgrad[PAD : PAD + per_dev]

    slots, seqs = returned.shape[0], tails.shape[1]
    per_seq = ctx.shape[0] // seqs
    rows = per_seq * SPAN
    at_start = arrived[slots] == 0
    for t, (ref, here) in enumerate(((ctx, context), (dq, query_grad))):
        for j in range(seqs):
            tail = tails[t, j].astype(F32)
            tail = jnp.where(at_start, jnp.zeros_like(tail), tail)
            first = slots + 1 + per_seq * j
            own = [ref[arrived[first + u]].astype(F32) for u in range(per_seq)]
            both = jnp.concatenate([tail] + own, axis=0)
            here[j] = pltpu.roll(both, rows + LAG, 0)[:rows].astype(BF)
    out[...] = jnp.zeros_like(out)
    for s in range(slots):
        row = arrived[s]
        part = returned[s].astype(F32)
        out[jnp.clip(row, 0, out.shape[0] - 1)] += jnp.where(row >= 0, part, jnp.zeros_like(part))


def local(n_dp, n_seq, queries, d_context, database, key_weight, value_weight, shard, wanted):
    nz, side = dims(n_dp, n_seq)
    seqs, span, width = queries.shape
    blocks = seqs * span // SPAN
    refs = blocks * shard.shape[-1]
    slots = n_dp * CAP
    enc = database.shape[2]
    vmem = pl.BlockSpec(memory_space=pltpu.VMEM)
    smem = pl.BlockSpec(memory_space=pltpu.SMEM)
    anywhere = pl.BlockSpec(memory_space=pl.ANY)
    dma = pltpu.SemaphoreType.DMA
    regular = pltpu.SemaphoreType.REGULAR
    rows_2 = PAD * nz
    chunks = 4
    chunk = 2 * width // chunks
    more = side - 1
    ctx, dq, tails, returned, arrived, wgrad = pl.pallas_call(
        functools.partial(main_kernel, nz, side),
        name="main",
        out_shape=(
            jax.ShapeDtypeStruct((blocks, SPAN, width), BF),
            jax.ShapeDtypeStruct((blocks, SPAN, width), BF),
            jax.ShapeDtypeStruct((2, seqs, SPAN, width), BF),
            jax.ShapeDtypeStruct((slots, NB_LEN, enc), BF),
            jax.ShapeDtypeStruct((slots + 1 + blocks,), jnp.int32),
            jax.ShapeDtypeStruct((2 * PAD, width), F32),
        ),
        in_specs=[smem, smem] + [anywhere] * 5,
        out_specs=(anywhere, anywhere, anywhere, anywhere, smem, vmem),
        scratch_shapes=[
            pltpu.VMEM((database.shape[0], NB_LEN, enc), BF),
            pltpu.VMEM((slots, NB_LEN, enc), BF),
            pltpu.VMEM((slots, NB_LEN, enc), BF),
            pltpu.VMEM((n_dp, 8, 128), jnp.int32),
            pltpu.VMEM((n_dp, 8, 128), jnp.int32),
            pltpu.SMEM((n_dp, 8, 128), jnp.int32),
            pltpu.VMEM((2, seqs, SPAN, width), BF),
            pltpu.VMEM((seqs, span, width), BF),
            pltpu.VMEM((seqs, span, width), BF),
            pltpu.VMEM((blocks, SPAN, width), BF),
            pltpu.VMEM((blocks, SPAN, width), BF),
            pltpu.VMEM((enc, width), BF),
            pltpu.VMEM((enc, width), BF),
            pltpu.VMEM((slots, NB_LEN, 2 * width), BF),
            pltpu.VMEM((refs, NB_LEN, 2 * width), BF),
            pltpu.VMEM((refs * NB_LEN, enc), F32),
            pltpu.VMEM((refs * NB_LEN, 2 * HD), BF),
            pltpu.VMEM((refs * NB_LEN, 2 * HD), BF),
            pltpu.VMEM((refs * NB_LEN, 2 * HD), BF),
            pltpu.VMEM((refs * NB_LEN, 2 * HD), BF),
            pltpu.VMEM((2, seqs, SPAN, width), BF),
            pltpu.VMEM((chunks, more, rows_2, chunk), BF),
            pltpu.VMEM((nz, 2 * PAD, width), BF),
            pltpu.VMEM((nz - 1, 2 * PAD, width), BF),
            dma((9,)),
            dma((n_dp,)),
            dma((n_dp,)),
            dma((CAP, n_dp)),
            dma((CAP, n_dp)),
            dma((2,)),
            dma((2,)),
            dma((CAP,)),
            dma((CAP, n_dp)),
            dma((CAP, n_dp)),
            dma((width // (4 * HD), 2, seqs)),
            dma((width // (4 * HD), 2, seqs)),
            dma((chunks,)),
            dma((chunks,)),
            dma((chunks, more)),
            dma((chunks, more)),
            dma((chunks, more)),
            dma((chunks, more)),
            dma((nz - 1,)),
            dma((nz - 1,)),
            regular,
            regular,
        ],
        compiler_params=pltpu.CompilerParams(
            collective_id=0, has_side_effects=True, vmem_limit_bytes=VMEM_LIMIT
        ),
    )(
        shard.swapaxes(2, 3),
        wanted.swapaxes(2, 3),
        database,
        queries,
        d_context,
        key_weight,
        value_weight,
    )
    rows = 32
    per_dev = enc // (n_dp * n_seq)
    part = jax.ShapeDtypeStruct((per_dev, width), F32)
    steps = NB_LEN // rows
    lanes = width // steps
    placed = jax.ShapeDtypeStruct(queries.shape, BF)
    database_grad, key_part, value_part, context, query_grad = pl.pallas_call(
        finish_kernel,
        name="finish",
        out_shape=(jax.ShapeDtypeStruct(database.shape, F32), part, part, placed, placed),
        grid_spec=pltpu.PrefetchScalarGridSpec(
            num_scalar_prefetch=1,
            grid=(steps,),
            in_specs=[
                pl.BlockSpec((slots, rows, enc), lambda i, s: (0, i, 0)),
                pl.BlockSpec((2 * PAD, width), lambda i, s: (0, 0)),
                pl.BlockSpec((blocks, SPAN, lanes), lambda i, s: (0, 0, i)),
                pl.BlockSpec((blocks, SPAN, lanes), lambda i, s: (0, 0, i)),
                pl.BlockSpec((2, seqs, SPAN, lanes), lambda i, s: (0, 0, 0, i)),
            ],
            out_specs=(
                pl.BlockSpec((database.shape[0], rows, enc), lambda i, s: (0, i, 0)),
                pl.BlockSpec((per_dev, width), lambda i, s: (0, 0)),
                pl.BlockSpec((per_dev, width), lambda i, s: (0, 0)),
                pl.BlockSpec((seqs, span, lanes), lambda i, s: (0, 0, i)),
                pl.BlockSpec((seqs, span, lanes), lambda i, s: (0, 0, i)),
            ),
        ),
        compiler_params=pltpu.CompilerParams(vmem_limit_bytes=VMEM_LIMIT),
    )(arrived, returned, wgrad, ctx, dq, tails)
    return context, query_grad, database_grad, key_part, value_part


def solution(mesh):
    return jax.shard_map(
        functools.partial(local, mesh.shape["dp"], mesh.shape["seq"]),
        mesh=mesh,
        in_specs=(
            P("dp", "seq", None),
            P("dp", "seq", None),
            P(("dp", "seq"), None, None),
            P(),
            P(),
            P("dp", "seq", None, None),
            P("dp", "seq", None, None),
        ),
        out_specs=(
            P("dp", "seq", None),
            P("dp", "seq", None),
            P(("dp", "seq"), None, None),
            P(("dp", "seq"), None),
            P(("dp", "seq"), None),
        ),
        check_vma=False,
    )
```

```python
import functools

import jax
import jax.numpy as jnp
from jax import lax
from jax.experimental import pallas as pl
from jax.experimental.pallas import tpu as pltpu
from jax.sharding import PartitionSpec as P

HD = 128
SPAN = 64
LAG = SPAN - 1
NB_LEN = 128
CAP = 2
PAD = 8
BF = jnp.bfloat16
F32 = jnp.float32
MESH = pl.DeviceIdType.MESH
VMEM_LIMIT = 62 * 2**20


def dims(n_dp, n_seq):
    side = int(round(n_seq**0.5))
    return n_dp // 2, side


def position():
    dp, seq = lax.axis_index("dp"), lax.axis_index("seq")
    return dp, seq, dp // 2, dp % 2


def toward(nz, rel):
    dp, seq, z, c = position()
    dz, dc = rel // 2, rel % 2
    return (lax.rem(z + dz, nz) * 2 + lax.rem(c + dc, 2), seq)


def back(nz, rel):
    dp, seq, z, c = position()
    dz, dc = rel // 2, rel % 2
    return (lax.rem(z + nz - dz, nz) * 2 + lax.rem(c + dc, 2), seq)


def along(side, first, step):
    dp, seq, z, c = position()
    y, x = seq // side, seq % side
    by_y = (1 - c) if first else c
    ny = lax.rem(y + step * by_y, side)
    nx = lax.rem(x + step * (1 - by_y), side)
    return (dp, ny * side + nx)


def greet(devices):
    barrier = pltpu.get_barrier_semaphore()
    for device in devices:
        pl.semaphore_signal(barrier, inc=1, device_id=device, device_id_type=MESH)
    pl.semaphore_wait(barrier, len(devices))


def remote(src, dst, send, recv, device):
    return pltpu.make_async_remote_copy(
        src_ref=src,
        dst_ref=dst,
        send_sem=send,
        recv_sem=recv,
        device_id=device,
        device_id_type=MESH,
    )


def far_first(nz):
    return sorted(range(2 * nz), key=lambda r: (-min(r // 2, nz - r // 2), r))


def nt(a, b):
    return lax.dot_general(a, b, (((1,), (1,)), ((), ())), preferred_element_type=F32)


def tn(a, b):
    return lax.dot_general(a, b, (((0,), (0,)), ((), ())), preferred_element_type=F32)


def nn(a, b):
    return jnp.dot(a, b, preferred_element_type=F32)


def main_kernel(
    nz, side,
    shard, wanted, db_hbm, q_hbm, g_hbm, kw_hbm, vw_hbm,
    ctx_out, dq_out, tails_out, returned, arrived, wgrad,
    db, outb, inb, req, arr, arr_s, heads, q, g, qs, gs, kw, vw, kv, pg, ng, sa_k, sa_v, sb_k, sb_v, tails,
    r2, s3, r3,
    ld, rq_s, rq_r, ga_s, ga_r, hd_s, hd_r, own_sem, rt_s, rt_r, tl_s, tl_r,
    p0_s, p0_r, p1_s, p1_r, p2_s, p2_r, p3_s, p3_r, free0, free1,
):
    n_seq = side * side
    dp, seq, z, c = position()
    y, x = seq // side, seq % side
    before = (dp, lax.rem(seq + n_seq - 1, n_seq))
    after = (dp, lax.rem(seq + 1, n_seq))
    sibling = (z * 2 + (1 - c), seq)
    rels = [r for r in far_first(nz) if r]
    steps = range(1, side)
    loads = []
    pairs_in = ((db_hbm, db), (kw_hbm, kw), (vw_hbm, vw), (q_hbm, q), (g_hbm, g))
    for i, (src, dst) in enumerate(pairs_in):
        copy = pltpu.make_async_copy(src, dst, ld.at[i])
        copy.start()
        loads.append(copy)
    picks, blocks = shard.shape[2], shard.shape[3]
    refs = blocks * picks
    near_by = 2 * nz
    slots = CAP * near_by
    named = [[shard[0, 0, i, b] for i in range(picks)] for b in range(blocks)]
    order = [jnp.int32(b) for b in range(blocks)]
    for e0 in reversed(range(blocks)):
        for e1 in reversed(range(e0 + 1, blocks)):
            apart = 0
            for i in named[e0]:
                for j in named[e1]:
                    apart = apart + jnp.where(i == j, 1, 0)
            wish = [e0, e1] + [b for b in range(blocks) if b not in (e0, e1)]
            order = [jnp.where(apart == 0, w, o) for w, o in zip(wish, order)]
    place = [
        sum([jnp.where(order[n] == b, n, 0) for n in range(blocks)], jnp.int32(0))
        for b in range(blocks)
    ]
    target = [shard[0, 0, i % picks, order[i // picks]] for i in range(refs)]
    row_of = [wanted[0, 0, i % picks, order[i // picks]] for i in range(refs)]
    slot = []
    for i in range(refs):
        rank = sum([jnp.where(target[j] == target[i], 1, 0) for j in range(i)], jnp.int32(0))
        dz = lax.rem(z + nz - target[i] // 2, nz)
        dc = lax.rem(c + target[i], 2)
        slot.append(jnp.minimum(rank, CAP - 1) * near_by + dz * 2 + dc)
    lane = lax.broadcasted_iota(jnp.int32, (8, 128), 1)
    source = {}
    for r in range(2 * nz):
        tile = jnp.zeros((8, 128), jnp.int32)
        for k in range(CAP):
            here = [slot[i] == k * near_by + r for i in range(refs)]
            asked = sum([jnp.where(here[i], row_of[i] + 1, 0) for i in range(refs)], jnp.int32(0))
            mine = sum([jnp.where(here[i], i, 0) for i in range(refs)], jnp.int32(0))
            source[k, r] = jnp.minimum(mine, refs - 1)
            tile = jnp.where(lane == k, asked - 1, tile)
        req[r] = tile
    greet(
        [toward(nz, r) for r in rels]
        + [along(side, True, s) for s in steps]
        + [along(side, False, s) for s in steps]
        + [before, after]
    )
    asks = []
    for r in rels:
        copy = remote(req.at[r], arr.at[r], rq_s.at[r], rq_r.at[r], back(nz, r))
        copy.start()
        asks.append(copy)
    arr[0] = req[0]
    head_copies = []
    for t, ref in enumerate((q_hbm, g_hbm)):
        copy = remote(ref.at[:, 0:SPAN], heads.at[t], hd_s.at[t], hd_r.at[t], before)
        copy.start()
        head_copies.append(copy)
    for copy in asks:
        copy.wait_recv()
    to_smem = pltpu.make_async_copy(arr, arr_s, ld.at[5])
    to_smem.start()
    loads[0].wait()
    to_smem.wait()
    last_row = db.shape[0] - 1
    sends = {}
    first_sent = [1] + [r for r in rels if r != 1]
    for k in range(CAP):
        for r in first_sent:
            here = k * near_by + r
            row = jnp.clip(arr_s[r, 0, k], 0, last_row)
            outb[here] = db[row]
            copy = remote(
                outb.at[here], inb.at[here], ga_s.at[k, r], ga_r.at[k, r], toward(nz, r)
            )
            if k == 0:
                copy.start()
            sends[k, r] = copy
    for k in range(CAP):
        row = jnp.clip(arr_s[0, 0, k], 0, last_row)
        inb[k * near_by] = db[row]
    for r in range(near_by):
        for k in range(CAP):
            arrived[k * near_by + r] = arr_s[r, 0, k]
    arrived[slots] = seq
    for b in range(blocks):
        arrived[slots + 1 + b] = place[b]
    enc = db.shape[2]
    half_rows = PAD * nz * n_seq
    rows_2 = PAD * nz
    rows_1 = rows_2 * side
    piece = NB_LEN
    per_dev = enc // (2 * nz * n_seq)
    pieces = 2 * half_rows // piece
    for a in range(pieces):
        m = lax.broadcasted_iota(jnp.int32, (piece, 128), 0) + a * piece
        core, rest = m // half_rows, m % half_rows
        a1, a2, mz, row = rest // rows_1, (rest // rows_2) % side, (rest // PAD) % nz, rest % PAD
        cell = jnp.where(core == 0, a1 * side + a2, a2 * side + a1)
        column = ((mz * 2 + core) * n_seq + cell) * per_dev + row
        column = jnp.where(row < per_dev, column, enc)
        for o in range(0, enc, 128):
            hit = lax.broadcasted_iota(jnp.int32, (piece, 128), 1) + o == column
            db[a, :, o : o + 128] = jnp.where(hit, 1.0, 0.0).astype(BF)
    at_end = seq == n_seq - 1
    width = 256
    seqs, rows = q.shape[0], q.shape[1]
    per_seq = rows // SPAN
    for t in range(2):
        loads[3 + t].wait()
        head_copies[t].wait_recv()
    for t, (ref, out) in enumerate(((q, qs), (g, gs))):
        for n in range(blocks):

            def shift(i, carry, ref=ref, out=out, t=t, n=n):
                lanes = pl.ds(pl.multiple_of(i * width, width), width)
                j, u = order[n] // per_seq, order[n] % per_seq
                own = ref[j, :, lanes].astype(F32)
                head = heads[t, j, :, lanes].astype(F32)
                head = jnp.where(at_end, jnp.zeros_like(head), head)
                both = jnp.concatenate([own, head], axis=0)
                moved = pltpu.roll(both, rows + SPAN - LAG, 0)
                chosen = moved[:SPAN]
                for v in range(1, per_seq):
                    chosen = jnp.where(u == v, moved[v * SPAN : (v + 1) * SPAN], chosen)
                out[n, :, lanes] = chosen.astype(BF)
                return carry

            lax.fori_loop(0, ref.shape[2] // width, shift, 0)
    hw = kw.shape[1]
    loads[1].wait()
    loads[2].wait()
    step_lanes = 512

    for r in first_sent:
        for k in range(1, CAP):
            sends[k - 1, r].wait_send()
            sends[k, r].start()

    def arrive(k):
        for m in [0] + sorted(range(1, nz), key=lambda m: (-min(m, nz - m), m)):
            for r in (2 * m, 2 * m + 1):
                if r:
                    sends[k, r].wait_recv()
            first = k * near_by + 2 * m
            pair_of = slice(first, first + 2)

            def project(i, carry, pair_of=pair_of):
                lanes = pl.ds(pl.multiple_of(i * step_lanes, step_lanes), step_lanes)
                later = pl.ds(pl.multiple_of(hw + i * step_lanes, step_lanes), step_lanes)
                rows_in = inb[pair_of].reshape(2 * NB_LEN, enc)
                keys = nn(rows_in, kw[:, lanes]).astype(BF)
                kv[pair_of, :, lanes] = keys.reshape(2, NB_LEN, step_lanes)
                values = nn(rows_in, vw[:, lanes]).astype(BF)
                kv[pair_of, :, later] = values.reshape(2, NB_LEN, step_lanes)
                return carry

            lax.fori_loop(0, hw // step_lanes, project, 0)

    scale = HD**-0.5
    wide = 2 * HD
    first_head = lax.broadcasted_iota(jnp.int32, (SPAN, wide), 1) < HD

    def diagonal(a):
        zero = jnp.zeros_like(a)
        return jnp.concatenate(
            [jnp.where(first_head, a, zero), jnp.where(first_head, zero, a)], axis=0
        )

    def folded(a):
        return jnp.where(first_head, a[:SPAN], a[SPAN:]).astype(BF)

    def attend(every, hp, stage_k, stage_v, beside):
        lanes = pl.ds(pl.multiple_of(hp * wide, wide), wide)
        later = pl.ds(pl.multiple_of(hw + hp * wide, wide), wide)
        kb, vb, qd, gd = {}, {}, {}, {}
        for b in every:
            mine = [slot[picks * b + i] for i in range(picks)]
            kb[b] = jnp.concatenate([kv[i, :, lanes] for i in mine], axis=0)
            vb[b] = jnp.concatenate([kv[i, :, later] for i in mine], axis=0)
            qd[b] = diagonal(qs[b, :, lanes])
            gd[b] = diagonal(gs[b, :, lanes])
        scores = {b: nt(qd[b], kb[b]) for b in every}
        pgr = {b: nt(gd[b], vb[b]) for b in every}
        beside(0)
        p = {}
        for b in every:
            e = jnp.exp(scores[b] * scale)
            p[b] = e / jnp.sum(e, axis=1, keepdims=True)
        half = {b: p[b].astype(BF) for b in every}
        beside(1)
        out = {b: folded(nn(half[b], vb[b])) for b in every}
        value_g = {b: tn(half[b], gd[b]).astype(BF) for b in every}
        beside(2)
        ds = {}
        for b in every:
            delta = jnp.sum(p[b] * pgr[b], axis=1, keepdims=True)
            ds[b] = (scale * p[b] * (pgr[b] - delta)).astype(BF)
        beside(3)
        back_out = {b: folded(nn(ds[b], kb[b])) for b in every}
        key_g = {b: tn(ds[b], qd[b]).astype(BF) for b in every}
        for b in every:
            rows_b = slice(b * picks * NB_LEN, (b + 1) * picks * NB_LEN)
            qs[b, :, lanes] = out[b]
            gs[b, :, lanes] = back_out[b]
            stage_k[rows_b] = key_g[b]
            stage_v[rows_b] = value_g[b]
            pg[picks * b : picks * (b + 1), :, lanes] = key_g[b].reshape(picks, NB_LEN, wide)
            pg[picks * b : picks * (b + 1), :, later] = value_g[b].reshape(picks, NB_LEN, wide)

    def add_near(every, hp, stage_k, stage_v):
        lanes = pl.ds(pl.multiple_of(hp * wide, wide), wide)

        def add(step):
            if step % 2 or step // 2 >= len(every):
                return
            b = every[step // 2]
            rows_b = slice(b * picks * NB_LEN, (b + 1) * picks * NB_LEN)
            ng[rows_b] += nt(stage_k[rows_b], kw[:, lanes]) + nt(stage_v[rows_b], vw[:, lanes])

        return add

    ng[...] = jnp.zeros_like(ng)
    sb_k[...] = jnp.zeros_like(sb_k)
    sb_v[...] = jnp.zeros_like(sb_v)

    def tail_copy(i, t, j):
        lanes = pl.ds(pl.multiple_of(i * 2 * wide, 2 * wide), 2 * wide)
        return remote(
            heads.at[t, j, :, lanes], tails.at[t, j, :, lanes],
            tl_s.at[i, t, j], tl_r.at[i, t, j], after,
        )

    def half_of(every, at_last):
        def two_pairs(i, carry):
            attend(
                every, 2 * i, sa_k, sa_v, add_near(every, jnp.maximum(2 * i - 1, 0), sb_k, sb_v)
            )
            attend(every, 2 * i + 1, sb_k, sb_v, add_near(every, 2 * i, sa_k, sa_v))
            if at_last:
                lanes = pl.ds(pl.multiple_of(i * 2 * wide, 2 * wide), 2 * wide)
                for t, ref in enumerate((qs, gs)):
                    for j in range(seqs):
                        heads[t, j, :, lanes] = ref[place[per_seq * (j + 1) - 1], :, lanes]
                        tail_copy(i, t, j).start()
            return carry

        lax.fori_loop(0, hw // (2 * wide), two_pairs, 0)
        last = add_near(every, hw // wide - 1, sb_k, sb_v)
        for step in range(2 * len(every)):
            last(step)

    for k in range(CAP):
        arrive(k)
        half_of([2 * k, 2 * k + 1], k == CAP - 1)
    for i in range(refs):
        db[pieces + i] = ng[i * NB_LEN : (i + 1) * NB_LEN].astype(BF)
    pl.semaphore_signal(free0, inc=1, device_id=sibling, device_id_type=MESH)
    for s in steps:
        pl.semaphore_signal(free1, inc=1, device_id=along(side, True, s), device_id_type=MESH)
    for r in rels:
        sends[CAP - 1, r].wait_send()
    return_copies = []

    def give_back(k, r):
        here = k * near_by + r
        outb[here] = db[pieces + source[k, r]]
        if r:
            copy = remote(
                outb.at[here], returned.at[here], rt_s.at[k, r], rt_r.at[k, r], back(nz, r)
            )
            return_copies.append(copy)
        else:
            copy = pltpu.make_async_copy(outb.at[here], returned.at[here], own_sem.at[k])
            own_copies.append(copy)
        copy.start()

    own_copies = []
    chunks = p0_s.shape[0]
    cw = 2 * hw // chunks
    my1 = jnp.where(c == 0, y, x)
    my2 = jnp.where(c == 0, x, y)
    phase0, phase1, phase2, phase3 = [], [], [], []

    def rows_of(a):
        return pl.ds(pl.multiple_of(a * rows_2, rows_2), rows_2)

    def lanes_of(a):
        return pl.ds(pl.multiple_of(a * cw, cw), cw)

    def product(core, i, base):
        start = pl.multiple_of(core * half_rows, half_rows)
        some = jnp.concatenate([part[pl.ds(start, half_rows)] for part in near_t], axis=1)
        for o in range(0, cw, step_lanes):
            these = pg[:, :, i * cw + o : i * cw + o + step_lanes]
            out = nn(some, these.reshape(refs * NB_LEN, step_lanes)).astype(BF)
            for a in range(side):
                kv[base + i, :, a * cw + o : a * cw + o + step_lanes] = out[
                    a * rows_1 : (a + 1) * rows_1
                ]

    def multiply(i):
        product(1 - c, i, 0)
        if i == 0:
            pl.semaphore_wait(free0, 1)
        copy = remote(kv.at[i], kv.at[2 * chunks + i], p0_s.at[i], p0_r.at[i], sibling)
        copy.start()
        phase0.append(copy)
        product(c, i, chunks)

    def send_first(i):
        phase0[i].wait_recv()
        kv[chunks + i] = (kv[chunks + i].astype(F32) + kv[2 * chunks + i].astype(F32)).astype(BF)
        if i == 0:
            pl.semaphore_wait(free1, side - 1)
        out = []
        for s in steps:
            to = lax.rem(my1 + s, side)
            copy = remote(
                kv.at[chunks + i, :, lanes_of(to)],
                kv.at[3 * chunks + i, :, pl.ds((s - 1) * cw, cw)],
                p1_s.at[i, s - 1], p1_r.at[i, s - 1], along(side, True, s),
            )
            copy.start()
            out.append(copy)
        phase1.append(out)

    for r in rels + [0]:
        for k in range(CAP):
            give_back(k, r)
    outs = []
    for t, (ref, hbm) in enumerate(((qs, ctx_out), (gs, dq_out))):
        copy = pltpu.make_async_copy(ref, hbm, ld.at[6 + t])
        copy.start()
        outs.append(copy)
    near_t = (sa_k, sa_v, sb_k, sb_v)
    for i in range(0, refs, 2):
        both = jnp.concatenate([inb[slot[i]], inb[slot[i + 1]]], axis=0)
        near_t[i // 2][...] = nt(db[0:pieces].reshape(2 * half_rows, enc), both).astype(BF)
    for i in range(chunks + 1):
        if i < chunks:
            multiply(i)
        if i:
            send_first(i - 1)
    tail_copies = [
        tail_copy(i, t, j)
        for t in range(2)
        for j in range(seqs)
        for i in range(hw // (2 * wide))
    ]
    for copy in tail_copies:
        copy.wait_recv()
    copy = pltpu.make_async_copy(tails, tails_out, ld.at[8])
    copy.start()
    outs.append(copy)
    for i in range(chunks):
        total = kv[chunks + i, :, lanes_of(my1)].astype(F32)
        for s in steps:
            phase1[i][s - 1].wait_recv()
            total = total + kv[3 * chunks + i, :, (s - 1) * cw : s * cw].astype(F32)
        kv[3 * chunks + i, :, (side - 1) * cw : side * cw] = total.astype(BF)
        out = []
        for s in steps:
            to = lax.rem(my2 + s, side)
            copy = remote(
                kv.at[3 * chunks + i, rows_of(to), pl.ds((side - 1) * cw, cw)], r2.at[i, s - 1], p2_s.at[i, s - 1], p2_r.at[i, s - 1],
                along(side, False, s),
            )
            copy.start()
            out.append(copy)
        phase2.append(out)
    totals = []
    for i in range(chunks):
        total = kv[3 * chunks + i, rows_of(my2), (side - 1) * cw : side * cw].astype(F32)
        for s in steps:
            phase2[i][s - 1].wait_recv()
            total = total + r2[i, s - 1].astype(F32)
        totals.append(total)
        if i >= chunks // 2:
            a = i - chunks // 2
            for part in range(nz):
                row = slice(part * PAD, (part + 1) * PAD)
                both = jnp.concatenate([totals[a][row], total[row]], axis=0)
                s3[part, :, a * cw : (a + 1) * cw] = both.astype(BF)
    for s in range(1, nz):
        copy = remote(
            s3.at[lax.rem(z + s, nz)], r3.at[s - 1], p3_s.at[s - 1], p3_r.at[s - 1],
            (lax.rem(z + s, nz) * 2 + c, seq),
        )
        copy.start()
        phase3.append(copy)
    total = s3[z].astype(F32)
    for s in range(1, nz):
        phase3[s - 1].wait_recv()
        total = total + r3[s - 1].astype(F32)
    wgrad[...] = total
    for copy in outs + own_copies:
        copy.wait()
    for copy in return_copies:
        copy.wait_recv()
    for copy in (
        asks + head_copies + return_copies + tail_copies + phase0
        + sum(phase1, []) + sum(phase2, []) + phase3
    ):
        copy.wait_send()


def finish_kernel(
    arrived, returned, wgrad, ctx, dq, tails, out, key_part, value_part, context, query_grad
):
    @pl.when(pl.program_id(0) == 0)
    def _():
        per_dev = key_part.shape[0]
        key_part[...] = wgrad[0:per_dev]
        value_part[...] = wgrad[PAD : PAD + per_dev]

    slots, seqs = returned.shape[0], tails.shape[1]
    per_seq = ctx.shape[0] // seqs
    rows = per_seq * SPAN
    at_start = arrived[slots] == 0
    for t, (ref, here) in enumerate(((ctx, context), (dq, query_grad))):
        for j in range(seqs):
            tail = tails[t, j].astype(F32)
            tail = jnp.where(at_start, jnp.zeros_like(tail), tail)
            first = slots + 1 + per_seq * j
            own = [ref[arrived[first + u]].astype(F32) for u in range(per_seq)]
            both = jnp.concatenate([tail] + own, axis=0)
            here[j] = pltpu.roll(both, rows + LAG, 0)[:rows].astype(BF)
    out[...] = jnp.zeros_like(out)
    for s in range(slots):
        row = arrived[s]
        part = returned[s].astype(F32)
        out[jnp.clip(row, 0, out.shape[0] - 1)] += jnp.where(row >= 0, part, jnp.zeros_like(part))


def local(n_dp, n_seq, queries, d_context, database, key_weight, value_weight, shard, wanted):
    nz, side = dims(n_dp, n_seq)
    seqs, span, width = queries.shape
    blocks = seqs * span // SPAN
    refs = blocks * shard.shape[-1]
    slots = n_dp * CAP
    enc = database.shape[2]
    vmem = pl.BlockSpec(memory_space=pltpu.VMEM)
    smem = pl.BlockSpec(memory_space=pltpu.SMEM)
    anywhere = pl.BlockSpec(memory_space=pl.ANY)
    dma = pltpu.SemaphoreType.DMA
    regular = pltpu.SemaphoreType.REGULAR
    rows_2 = PAD * nz
    chunks = 4
    chunk = 2 * width // chunks
    more = side - 1
    ctx, dq, tails, returned, arrived, wgrad = pl.pallas_call(
        functools.partial(main_kernel, nz, side),
        name="main",
        out_shape=(
            jax.ShapeDtypeStruct((blocks, SPAN, width), BF),
            jax.ShapeDtypeStruct((blocks, SPAN, width), BF),
            jax.ShapeDtypeStruct((2, seqs, SPAN, width), BF),
            jax.ShapeDtypeStruct((slots, NB_LEN, enc), BF),
            jax.ShapeDtypeStruct((slots + 1 + blocks,), jnp.int32),
            jax.ShapeDtypeStruct((2 * PAD, width), F32),
        ),
        in_specs=[smem, smem] + [anywhere] * 5,
        out_specs=(anywhere, anywhere, anywhere, anywhere, smem, vmem),
        scratch_shapes=[
            pltpu.VMEM((database.shape[0], NB_LEN, enc), BF),
            pltpu.VMEM((slots, NB_LEN, enc), BF),
            pltpu.VMEM((slots, NB_LEN, enc), BF),
            pltpu.VMEM((n_dp, 8, 128), jnp.int32),
            pltpu.VMEM((n_dp, 8, 128), jnp.int32),
            pltpu.SMEM((n_dp, 8, 128), jnp.int32),
            pltpu.VMEM((2, seqs, SPAN, width), BF),
            pltpu.VMEM((seqs, span, width), BF),
            pltpu.VMEM((seqs, span, width), BF),
            pltpu.VMEM((blocks, SPAN, width), BF),
            pltpu.VMEM((blocks, SPAN, width), BF),
            pltpu.VMEM((enc, width), BF),
            pltpu.VMEM((enc, width), BF),
            pltpu.VMEM((slots, NB_LEN, 2 * width), BF),
            pltpu.VMEM((refs, NB_LEN, 2 * width), BF),
            pltpu.VMEM((refs * NB_LEN, enc), F32),
            pltpu.VMEM((refs * NB_LEN, 2 * HD), BF),
            pltpu.VMEM((refs * NB_LEN, 2 * HD), BF),
            pltpu.VMEM((refs * NB_LEN, 2 * HD), BF),
            pltpu.VMEM((refs * NB_LEN, 2 * HD), BF),
            pltpu.VMEM((2, seqs, SPAN, width), BF),
            pltpu.VMEM((chunks, more, rows_2, chunk), BF),
            pltpu.VMEM((nz, 2 * PAD, width), BF),
            pltpu.VMEM((nz - 1, 2 * PAD, width), BF),
            dma((9,)),
            dma((n_dp,)),
            dma((n_dp,)),
            dma((CAP, n_dp)),
            dma((CAP, n_dp)),
            dma((2,)),
            dma((2,)),
            dma((CAP,)),
            dma((CAP, n_dp)),
            dma((CAP, n_dp)),
            dma((width // (4 * HD), 2, seqs)),
            dma((width // (4 * HD), 2, seqs)),
            dma((chunks,)),
            dma((chunks,)),
            dma((chunks, more)),
            dma((chunks, more)),
            dma((chunks, more)),
            dma((chunks, more)),
            dma((nz - 1,)),
            dma((nz - 1,)),
            regular,
            regular,
        ],
        compiler_params=pltpu.CompilerParams(
            collective_id=0, has_side_effects=True, vmem_limit_bytes=VMEM_LIMIT
        ),
    )(
        shard.swapaxes(2, 3),
        wanted.swapaxes(2, 3),
        database,
        queries,
        d_context,
        key_weight,
        value_weight,
    )
    rows = 32
    per_dev = enc // (n_dp * n_seq)
    part = jax.ShapeDtypeStruct((per_dev, width), F32)
    steps = NB_LEN // rows
    lanes = width // steps
    placed = jax.ShapeDtypeStruct(queries.shape, BF)
    database_grad, key_part, value_part, context, query_grad = pl.pallas_call(
        finish_kernel,
        name="finish",
        out_shape=(jax.ShapeDtypeStruct(database.shape, F32), part, part, placed, placed),
        grid_spec=pltpu.PrefetchScalarGridSpec(
            num_scalar_prefetch=1,
            grid=(steps,),
            in_specs=[
                pl.BlockSpec((slots, rows, enc), lambda i, s: (0, i, 0)),
                pl.BlockSpec((2 * PAD, width), lambda i, s: (0, 0)),
                pl.BlockSpec((blocks, SPAN, lanes), lambda i, s: (0, 0, i)),
                pl.BlockSpec((blocks, SPAN, lanes), lambda i, s: (0, 0, i)),
                pl.BlockSpec((2, seqs, SPAN, lanes), lambda i, s: (0, 0, 0, i)),
            ],
            out_specs=(
                pl.BlockSpec((database.shape[0], rows, enc), lambda i, s: (0, i, 0)),
                pl.BlockSpec((per_dev, width), lambda i, s: (0, 0)),
                pl.BlockSpec((per_dev, width), lambda i, s: (0, 0)),
                pl.BlockSpec((seqs, span, lanes), lambda i, s: (0, 0, i)),
                pl.BlockSpec((seqs, span, lanes), lambda i, s: (0, 0, i)),
            ),
        ),
        compiler_params=pltpu.CompilerParams(vmem_limit_bytes=VMEM_LIMIT),
    )(arrived, returned, wgrad, ctx, dq, tails)
    return context, query_grad, database_grad, key_part, value_part


def solution(mesh):
    return jax.shard_map(
        functools.partial(local, mesh.shape["dp"], mesh.shape["seq"]),
        mesh=mesh,
        in_specs=(
            P("dp", "seq", None),
            P("dp", "seq", None),
            P(("dp", "seq"), None, None),
            P(),
            P(),
            P("dp", "seq", None, None),
            P("dp", "seq", None, None),
        ),
        out_specs=(
            P("dp", "seq", None),
            P("dp", "seq", None),
            P(("dp", "seq"), None, None),
            P(("dp", "seq"), None),
            P(("dp", "seq"), None),
        ),
        check_vma=False,
    )
```
